512 devices in a mesh: shot: 64 (over x, z, y_lo), strip: 8 (over y_hi, core).
Axes of the slice: x: 4, y: 8 (y_hi: 4, y_lo: 2; y = y_hi * 2 + y_lo), z: 8, core: 2. Of those that a mesh axis runs over, the one named last changes fastest.
Arguments:
- source_field: bfloat16 [64, 16, 8, 16, 1024], P('shot', None, None, None, 'strip'), may hold values from -6 to 6
- receiver_field: bfloat16 [64, 16, 8, 16, 1024], P('shot', None, None, None, 'strip'), may hold values from -6 to 6
- shot_pos: int32 [64], P('shot'), may hold values from 0 to 1023
- offset_weight: int32 [33], replicated, may hold values from 1 to 16
Outputs:
- source_update: float32 [64, 16, 8, 16, 1024], P('shot', None, None, None, 'strip')
- receiver_update: float32 [64, 16, 8, 16, 1024], P('shot', None, None, None, 'strip')
The draws below stay inside these ranges and needn't reach their ends.
All inputs are finite; a program needn't handle non-finite values.
Results may differ from the reference program's by a relative error of at most 0.0003.
Values may be sent and summed in bfloat16 or wider, within the bound.
A program may use at most 64 MiB of HBM per device.

```python
import jax
import jax.numpy as jnp
from jax import lax

NT = 16
NZ = 8
HOFF = 16
NOFF = 33
NY = 16
NSHOT = 64
NX = 1024


def with_ends(drawn, own_key, smallest, largest):
    index_at = [jax.random.randint(jax.random.fold_in(own_key, axis), (), 0, length) for axis, length in enumerate(drawn.shape)]
    widest = drawn.shape.index(max(drawn.shape))
    next_to = index_at[:widest] + [(index_at[widest] + 1) % drawn.shape[widest]] + index_at[widest + 1:]
    return drawn.at[tuple(index_at)].set(smallest).at[tuple(next_to)].set(largest)


def levels(own_key, dims, pieces, smallest, largest):
    gain = 1.0
    for dim, shards_of in pieces:
        steps = jax.random.uniform(jax.random.fold_in(jax.random.fold_in(own_key, 6), dim), (shards_of,), jnp.float32, smallest / len(pieces), largest / len(pieces))
        gain = gain * jnp.repeat(jnp.exp(steps), dims[dim] // shards_of).reshape((-1,) + (1,) * (len(dims) - 1 - dim))
    return gain


def normal_values(own_key, extent, scale, bound, cuts=(), held_as=jnp.bfloat16):
    entries = scale * jax.random.normal(own_key, extent, jnp.float32)
    if cuts:
        entries = entries * levels(own_key, extent, cuts, -0.22, 0.18)
    return jnp.clip(entries, -bound, bound).astype(held_as)


def setup_inputs(seed: int = 0) -> dict:
    seeds = jax.random.split(jax.random.key(seed), 5)
    source_field = normal_values(seeds[0], (NSHOT, NT, NZ, NY, NX), 1.0, 6.0, ((0, 64), (4, 8)))
    receiver_field = normal_values(seeds[1], (NSHOT, NT, NZ, NY, NX), 1.0, 6.0, ((0, 64), (4, 8)))
    shot_pos = with_ends(jax.random.randint(seeds[2], (NSHOT,), 0, NX), jax.random.fold_in(seeds[2], 1), 0, NX - 1).astype(jnp.int32)
    offset_weight = with_ends(jax.random.randint(seeds[3], (NOFF,), 1, 17), jax.random.fold_in(seeds[3], 1), 1, 16).astype(jnp.int32)
    return dict(source_field=source_field, receiver_field=receiver_field, shot_pos=shot_pos, offset_weight=offset_weight)


def reference(source_field, receiver_field, shot_pos, offset_weight):
    nshot = source_field.shape[0]
    width = source_field.shape[-1]
    cells = jnp.arange(width, dtype=jnp.int32)
    apert = width // 4
    pads = ((0, 0), (0, 0), (0, 0), (HOFF, HOFF))

    def masking(src, pos):
        inside = jnp.abs(cells - pos) <= apert
        return jnp.where(inside, src, jnp.zeros_like(src)), inside

    def add_shot(total, item):
        src, rec, pos = item
        masked, inside = masking(src, pos)
        padded = jnp.pad(rec, pads)
        terms = [jnp.sum(masked.astype(jnp.float32) * padded[..., k:k + width].astype(jnp.float32), axis=0) for k in range(NOFF)]
        return total + jnp.stack(terms), None

    start = jnp.zeros((NOFF, NZ, NY, width), jnp.float32)
    image, unused = lax.scan(add_shot, start, (source_field, receiver_field, shot_pos))
    penalty = offset_weight.astype(jnp.float32)[:, None, None, None] * image / float(nshot * NT)
    penalty_pad = jnp.pad(penalty, ((0, 0), (0, 0), (0, 0), (HOFF, HOFF)))

    def back(item):
        src, rec, pos = item
        masked, inside = masking(src, pos)
        rec_pad = jnp.pad(rec, pads).astype(jnp.float32)
        src_pad = jnp.pad(masked, pads).astype(jnp.float32)
        src_upd = jnp.zeros((NT, NZ, NY, width), jnp.float32)
        rec_upd = jnp.zeros((NT, NZ, NY, width), jnp.float32)
        for k in range(NOFF):
            src_upd = src_upd + penalty[k] * rec_pad[..., k:k + width]
            lo = 2 * HOFF - k
            rec_upd = rec_upd + penalty_pad[k][..., lo:lo + width] * src_pad[..., lo:lo + width]
        src_upd = jnp.where(inside, src_upd, jnp.zeros_like(src_upd))
        return src_upd, rec_upd

    source_update, receiver_update = lax.map(back, (source_field, receiver_field, shot_pos))
    return (source_update, receiver_update)
```

```python
import functools

import jax
import jax.numpy as jnp
from jax import lax
from jax.experimental import pallas as pl
from jax.experimental.pallas import tpu as pltpu
from jax.sharding import PartitionSpec as P

MESH = pl.DeviceIdType.MESH
VMEM = pl.BlockSpec(memory_space=pltpu.VMEM)
SMEM = pl.BlockSpec(memory_space=pltpu.SMEM)
F32 = jnp.float32

NUM_X, NUM_Z, NUM_Y = 4, 8, 2
ROWS = 8
PAD = 36
QUARTER = PAD // 4
params = functools.partial(pltpu.CompilerParams, vmem_limit_bytes=56 * 2**20)


def prepare_kernel(strips, shots_pos, rec, src, rec_ext, src_ext, send, recv):
    steps, width = rec.shape[0], rec.shape[-1]
    rim = (rec_ext.shape[1] - width) // 2
    strip = lax.axis_index("strip")
    left, right = lax.rem(strip + strips - 1, strips), lax.rem(strip + 1, strips)
    barrier = pltpu.get_barrier_semaphore()
    for other in (left, right):
        pl.semaphore_signal(barrier, inc=1, device_id={"strip": other}, device_id_type=MESH)
    pos = shots_pos[0]
    cells = strip * width + lax.broadcasted_iota(jnp.int32, (width, width), 0)
    inside = jnp.abs(cells - pos) <= width * strips // 4

    @pl.loop(0, steps)
    def _(t):
        r = rec[t].reshape(width, width).astype(F32).T
        rec_ext[t, rim : rim + width] = r.astype(jnp.bfloat16)
        s = src[t].reshape(width, width).astype(F32).T
        src_ext[t, rim : rim + width] = jnp.where(inside, s, 0.0).astype(jnp.bfloat16)

    pl.semaphore_wait(barrier, 2)
    copies = []
    for i, ext in enumerate((rec_ext, src_ext)):
        copies.append(
            pltpu.make_async_remote_copy(
                src_ref=ext.at[:, width : width + rim],
                dst_ref=ext.at[:, 0:rim],
                send_sem=send.at[2 * i],
                recv_sem=recv.at[2 * i],
                device_id={"strip": right},
                device_id_type=MESH,
            )
        )
        copies.append(
            pltpu.make_async_remote_copy(
                src_ref=ext.at[:, rim : 2 * rim],
                dst_ref=ext.at[:, rim + width : 2 * rim + width],
                send_sem=send.at[2 * i + 1],
                recv_sem=recv.at[2 * i + 1],
                device_id={"strip": left},
                device_id_type=MESH,
            )
        )
    for copy in copies:
        copy.start()
    for copy in copies:
        copy.wait()
    has_left = jnp.full((rim, width), strip, jnp.int32) > 0
    has_right = jnp.full((rim, width), strip, jnp.int32) < strips - 1

    @pl.loop(0, steps)
    def _(t):
        for ext in (rec_ext, src_ext):
            low = ext[t, 0:rim].astype(F32)
            ext[t, 0:rim] = jnp.where(has_left, low, 0.0).astype(jnp.bfloat16)
            high = ext[t, rim + width : 2 * rim + width].astype(F32)
            ext[t, rim + width : 2 * rim + width] = jnp.where(has_right, high, 0.0).astype(jnp.bfloat16)


def image_kernel(terms, weight, rec_ext, src_ext, image, rec32, src32):
    steps, span, lanes = rec_ext.shape
    count = weight.shape[0]
    rim = count // 2

    @pl.loop(0, steps)
    def _(t):
        rec32[t] = rec_ext[t].astype(F32)
        src32[t] = src_ext[t].astype(F32)

    scale = [weight[k].astype(F32) * (1.0 / terms) for k in range(count)]

    @pl.loop(0, image.shape[0])
    def _(g):
        base = pl.multiple_of(g * ROWS, ROWS)
        own = [src32[t, pl.ds(base + rim, ROWS)] for t in range(steps)]
        for k in range(count):
            total = own[0] * rec32[0, pl.ds(base + k, ROWS)]
            for t in range(1, steps):
                total += own[t] * rec32[t, pl.ds(base + k, ROWS)]
            image[g, k] = total * scale[k]
        for k in range(count, PAD):
            image[g, k] = jnp.zeros((ROWS, lanes), F32)


def ring_chains(n):
    return ((1, n // 2, 0), (-1, n // 2 - 1, 0), (-1, n // 2, 1), (1, n // 2 - 1, 1))


def reduce_kernel(strips, count, img, out, slot_a, slot_b, acc_a, acc_b, in_a, in_b, in_y, fin, send, recv):
    shot, strip = lax.axis_index("shot"), lax.axis_index("strip")
    x, z, y = shot // (NUM_Z * NUM_Y), shot // NUM_Y % NUM_Z, shot % NUM_Y
    half_k = PAD // 2

    def at_x(i):
        return {"shot": (i * NUM_Z + z) * NUM_Y + y}

    def at_z(i):
        return {"shot": (x * NUM_Z + i) * NUM_Y + y}

    def wrap(i, n):
        return lax.rem(i + n, n)

    pair = {"shot": shot + 1 - 2 * y}
    left, right = {"strip": wrap(strip - 1, strips)}, {"strip": wrap(strip + 1, strips)}
    others = [at_x(wrap(x + d, NUM_X)) for d in range(1, NUM_X)]
    others += [at_z(wrap(z + d, NUM_Z)) for d in range(1, NUM_Z)]
    others += [pair, left, right]
    barrier = pltpu.get_barrier_semaphore()
    for other in others:
        pl.semaphore_signal(barrier, inc=1, device_id=other, device_id_type=MESH)
    pl.semaphore_wait(barrier, len(others))

    started = []

    def push(src_ref, dst_ref, device):
        i = len(started)
        copy = pltpu.make_async_remote_copy(
            src_ref=src_ref,
            dst_ref=dst_ref,
            send_sem=send.at[i],
            recv_sem=recv.at[i],
            device_id=device,
            device_id_type=MESH,
        )
        copy.start()
        started.append(copy)
        return copy

    def group_a(i):
        return i + (i // (NUM_Z // 2)) * 2 * NUM_X

    def group_b(i, half):
        return NUM_Z // 2 + 2 * i + half

    def part_a(ref, owner, half):
        return ref.at[group_a(owner), pl.ds(half * half_k, half_k)]

    def part_b(ref, owner, half):
        return ref.at[group_b(owner, half)]

    plans = {
        "a": (NUM_Z, z, at_z, part_a, slot_a),
        "b": (NUM_X, x, at_x, part_b, slot_b),
    }
    arrived = {}
    slots = {}
    for name, (n, *_) in plans.items():
        first = 0
        for c, (_, hops, _) in enumerate(ring_chains(n)):
            slots[name, c] = first
            first += hops

    def reduce_step(name, j):
        n, here, device, part, slot = plans[name]
        for c, (way, hops, half) in enumerate(ring_chains(n)):
            if j > hops:
                continue
            owner = wrap(here + way * (hops + 1 - j), n)
            mine = part(img, owner, half)
            if j > 1:
                held = slot.at[slots[name, c] + j - 2]
                arrived[name, c].wait_recv()
                held[...] += mine[...]
                mine = held
            arrived[name, c] = push(mine, slot.at[slots[name, c] + j - 1], device(wrap(here + way, n)))

    def reduce_end(name, store):
        n, here, _, part, slot = plans[name]
        chains = ring_chains(n)
        for half in range(2):
            total = part(img, here, half)[...]
            for c, (_, hops, side) in enumerate(chains):
                if side == half:
                    arrived[name, c].wait_recv()
                    total += slot[slots[name, c] + hops - 1]
            store(half, total)

    def store_a(half, total):
        acc_a[half * half_k : (half + 1) * half_k] = total

    def store_b(half, total):
        acc_b[half] = total

    def piece_b(ref, i):
        return ref.at[i // 4, pl.ds(i % 4 * QUARTER, QUARTER)]

    reduce_step("a", 1)
    reduce_step("b", 1)
    reduce_step("a", 2)
    reduce_step("b", 2)
    reduce_end("b", store_b)
    second_b = []
    for d in range(1, NUM_Z):
        other = wrap(z + d, NUM_Z)
        second_b.append(push(piece_b(acc_b, other), in_b.at[d - 1], at_z(other)))
    reduce_step("a", 3)
    reduce_step("a", 4)
    reduce_end("a", store_a)
    second_a = []
    for d in range(1, NUM_X):
        other = wrap(x + d, NUM_X)
        second_a.append(push(acc_a.at[pl.ds(other * QUARTER, QUARTER)], in_a.at[d - 1], at_x(other)))

    total = piece_b(acc_b, z)[...]
    for d in range(1, NUM_Z):
        second_b[d - 1].wait_recv()
        total += in_b[d - 1]
    fin[1] = total
    pair_b = push(fin.at[1], in_y.at[1], pair)
    total = acc_a[pl.ds(x * QUARTER, QUARTER)]
    for d in range(1, NUM_X):
        second_a[d - 1].wait_recv()
        total += in_a[d - 1]
    fin[0] = total
    pair_a = push(fin.at[0], in_y.at[0], pair)

    mine_b = out.at[group_b(x, z // 4), pl.ds(z % 4 * QUARTER, QUARTER)]
    pair_b.wait_recv()
    mine_b[...] = fin[1] + in_y[1]
    third_b = [push(mine_b, mine_b, at_z(wrap(z + d, NUM_Z))) for d in range(1, NUM_Z)]
    mine_a = out.at[group_a(z), pl.ds(x * QUARTER, QUARTER)]
    pair_a.wait_recv()
    mine_a[...] = fin[0] + in_y[0]
    third_a = [push(mine_a, mine_a, at_x(wrap(x + d, NUM_X))) for d in range(1, NUM_X)]

    def gather_step(name, j):
        n, here, device, part, _ = plans[name]
        for c, (way, hops, half) in enumerate(ring_chains(n)):
            if j > hops + 1:
                continue
            if j > 1:
                arrived[name, c].wait_recv()
            if j <= hops:
                held = part(out, wrap(here - way * (j - 1), n), half)
                arrived[name, c] = push(held, held, device(wrap(here + way, n)))

    for copy in third_b:
        copy.wait_recv()
    gather_step("b", 1)
    for copy in third_a:
        copy.wait_recv()
    gather_step("a", 1)
    gather_step("b", 2)
    gather_step("a", 2)
    gather_step("b", 3)
    gather_step("a", 3)
    gather_step("a", 4)
    gather_step("a", 5)

    rim = count // 2
    groups = img.shape[0]
    edge = rim // ROWS
    to_right = push(
        out.at[pl.ds(groups - edge, edge), pl.ds(rim + 1, rim)],
        out.at[pl.ds(groups, edge), pl.ds(rim + 1, rim)],
        right,
    )
    to_left = push(out.at[pl.ds(0, edge), pl.ds(0, rim)], out.at[pl.ds(groups + edge, edge), pl.ds(0, rim)], left)
    to_right.wait_recv()
    to_left.wait_recv()
    for copy in started:
        copy.wait_send()


def update_kernel(strips, shots_pos, rec_ext, src_ext, penalty, src_upd, rec_upd, rec32, src32, pen, held):
    steps, span, lanes = rec_ext.shape
    width = lanes
    rim = (span - width) // 2
    count = 2 * rim + 1
    groups = width // ROWS
    edge = rim // ROWS
    strip = lax.axis_index("strip")
    pos = shots_pos[0]

    @pl.loop(0, steps)
    def _(t):
        rec32[t] = rec_ext[t].astype(F32)
        src32[t] = src_ext[t].astype(F32)

    @pl.loop(0, count)
    def _(k):
        for g in range(groups):
            pen[k, rim + g * ROWS : rim + (g + 1) * ROWS] = penalty[g, k]
        for g in range(edge):
            pen[k, g * ROWS : (g + 1) * ROWS] = penalty[groups + g, k]
            start = rim + width + g * ROWS
            pen[k, start : start + ROWS] = penalty[groups + edge + g, k]

    @pl.loop(0, groups)
    def _(g):
        base = pl.multiple_of(g * ROWS, ROWS)
        cells = strip * width + base + lax.broadcasted_iota(jnp.int32, (ROWS, lanes), 0)
        inside = jnp.abs(cells - pos) <= width * strips // 4
        total = [jnp.zeros((ROWS, lanes), F32)] * steps
        for k in range(count):
            p = pen[k, pl.ds(base + rim, ROWS)]
            total = [total[t] + p * rec32[t, pl.ds(base + k, ROWS)] for t in range(steps)]
        for t in range(steps):
            held[t, pl.ds(base, ROWS)] = jnp.where(inside, total[t], 0.0)

    @pl.loop(0, steps)
    def _(t):
        src_upd[t] = held[t].T.reshape(src_upd.shape[1:])

    @pl.loop(0, groups)
    def _(g):
        base = pl.multiple_of(g * ROWS, ROWS)
        total = [jnp.zeros((ROWS, lanes), F32)] * steps
        for k in range(count):
            low = base + 2 * rim - k
            p = pen[k, pl.ds(low, ROWS)]
            total = [total[t] + p * src32[t, pl.ds(low, ROWS)] for t in range(steps)]
        for t in range(steps):
            held[t, pl.ds(base, ROWS)] = total[t]

    @pl.loop(0, steps)
    def _(t):
        rec_upd[t] = held[t].T.reshape(rec_upd.shape[1:])


def reduce_call(strips, count, image):
    groups, _, _, width = image.shape
    rim = count // 2
    quarter = (QUARTER, ROWS, width)
    return pl.pallas_call(
        functools.partial(reduce_kernel, strips, count),
        out_shape=jax.ShapeDtypeStruct((groups + 2 * rim // ROWS, PAD, ROWS, width), F32),
        in_specs=[VMEM],
        out_specs=VMEM,
        scratch_shapes=[
            pltpu.VMEM((2 * NUM_Z - 2, PAD // 2, ROWS, width), F32),
            pltpu.VMEM((2 * NUM_X - 2, PAD, ROWS, width), F32),
            pltpu.VMEM((PAD, ROWS, width), F32),
            pltpu.VMEM((2, PAD, ROWS, width), F32),
            pltpu.VMEM((NUM_X - 1,) + quarter, F32),
            pltpu.VMEM((NUM_Z - 1,) + quarter, F32),
            pltpu.VMEM((2,) + quarter, F32),
            pltpu.VMEM((2,) + quarter, F32),
            pltpu.SemaphoreType.DMA((64,)),
            pltpu.SemaphoreType.DMA((64,)),
        ],
        compiler_params=params(collective_id=1, has_side_effects=True),
        name="reduce",
    )(image)


def local(strips, shots, source_field, receiver_field, shot_pos, offset_weight):
    src, rec = source_field[0], receiver_field[0]
    steps, depth, lateral, width = src.shape
    count = offset_weight.shape[0]
    rim = count // 2
    span = width + 2 * rim
    groups = width // ROWS

    ext = jax.ShapeDtypeStruct((steps, span, width), jnp.bfloat16)
    rec_ext, src_ext = pl.pallas_call(
        functools.partial(prepare_kernel, strips),
        out_shape=(ext, ext),
        in_specs=[SMEM, VMEM, VMEM],
        out_specs=(VMEM, VMEM),
        scratch_shapes=[pltpu.SemaphoreType.DMA((4,)), pltpu.SemaphoreType.DMA((4,))],
        compiler_params=params(collective_id=0, has_side_effects=True),
        name="prepare",
    )(shot_pos, rec, src)

    wide = pltpu.VMEM((steps, span, width), F32)
    image = pl.pallas_call(
        functools.partial(image_kernel, float(shots * steps)),
        out_shape=jax.ShapeDtypeStruct((groups, PAD, ROWS, width), F32),
        in_specs=[SMEM, VMEM, VMEM],
        out_specs=VMEM,
        scratch_shapes=[wide, wide],
        compiler_params=params(),
        name="image",
    )(offset_weight, rec_ext, src_ext)

    penalty = reduce_call(strips, count, image)

    upd = jax.ShapeDtypeStruct(src.shape, F32)
    src_upd, rec_upd = pl.pallas_call(
        functools.partial(update_kernel, strips),
        out_shape=(upd, upd),
        in_specs=[SMEM, VMEM, VMEM, VMEM],
        out_specs=(VMEM, VMEM),
        scratch_shapes=[
            wide,
            wide,
            pltpu.VMEM((count, span, width), F32),
            pltpu.VMEM((steps, width, width), F32),
        ],
        compiler_params=params(),
        name="update",
    )(shot_pos, rec_ext, src_ext, penalty)
    return src_upd[None], rec_upd[None]


def solution(mesh):
    return jax.shard_map(
        functools.partial(local, mesh.shape["strip"], mesh.shape["shot"]),
        mesh=mesh,
        in_specs=(
            P("shot", None, None, None, "strip"),
            P("shot", None, None, None, "strip"),
            P("shot"),
            P(),
        ),
        out_specs=(P("shot", None, None, None, "strip"), P("shot", None, None, None, "strip")),
        check_vma=False,
    )
```

```python
import functools

import jax
import jax.numpy as jnp
from jax import lax
from jax.experimental import pallas as pl
from jax.experimental.pallas import tpu as pltpu
from jax.sharding import PartitionSpec as P

MESH = pl.DeviceIdType.MESH
VMEM = pl.BlockSpec(memory_space=pltpu.VMEM)
SMEM = pl.BlockSpec(memory_space=pltpu.SMEM)
F32 = jnp.float32

NUM_X, NUM_Z, NUM_Y = 4, 8, 2
ROWS = 8
BATCH, SOME = 4, 8
PAD = 36
QUARTER = PAD // 4
WORDS = (QUARTER + 1) // 2
TINY, LIMIT, STEPS_2 = 1e-30, 32767.0, 16.0


def unit_matrix(rows, columns):
    i = lax.broadcasted_iota(jnp.int32, (rows, columns), 0)
    j = lax.broadcasted_iota(jnp.int32, (rows, columns), 1)
    return jnp.where(lax.rem(j, rows) == i, 1.0, 0.0).astype(jnp.bfloat16)


def turned(unit, values):
    return lax.dot_general(unit, values, (((1,), (1,)), ((), ())), preferred_element_type=F32)


def turned_pair(unit, values):
    high = values.astype(jnp.bfloat16)
    low = (values - high.astype(F32)).astype(jnp.bfloat16)
    return turned(unit, jnp.concatenate([high, low], axis=1))


def encode(values):
    top = jnp.maximum(jnp.max(jnp.abs(values), axis=0), TINY)
    code = jnp.ceil(jnp.log2(top) * STEPS_2)
    scaled = jnp.round(values * (LIMIT / jnp.exp2(code * (1.0 / STEPS_2))))
    whole = jnp.clip(scaled, -LIMIT, LIMIT).astype(jnp.int32)
    low = jnp.concatenate([whole[WORDS:], code.astype(jnp.int32)[None]])
    return (whole[:WORDS] << 16) | (low & 0xFFFF)


def decode(words):
    high, low = words >> 16, (words << 16) >> 16
    scale = jnp.exp2(low[WORDS - 1].astype(F32) * (1.0 / STEPS_2)) * (1.0 / LIMIT)
    return jnp.concatenate([high, low[: WORDS - 1]]).astype(F32) * scale


def ring_chains(n):
    return ((1, n // 2, 0), (-1, n // 2 - 1, 0), (-1, n // 2, 1), (1, n // 2 - 1, 1))


def fused_kernel(
    strips,
    terms_count,
    shots_pos,
    weight,
    rec,
    src,
    src_upd,
    rec_upd,
    rec32,
    src32,
    edge_out,
    edge_in,
    img,
    out,
    pen,
    held,
    stage_z,
    stage_x,
    slot_z,
    slot_x,
    send_z,
    send_x,
    in_z,
    in_x,
    pair_out,
    pair_in,
    send,
    recv,
):
    steps, width = rec.shape[0], rec.shape[-1]
    count = weight.shape[0]
    rim = count // 2
    edge = rim // ROWS
    groups = width // ROWS
    shot, strip = lax.axis_index("shot"), lax.axis_index("strip")
    x, z, y = shot // (NUM_Z * NUM_Y), shot // NUM_Y % NUM_Z, shot % NUM_Y

    def at_x(i):
        return {"shot": (i * NUM_Z + z) * NUM_Y + y}

    def at_z(i):
        return {"shot": (x * NUM_Z + i) * NUM_Y + y}

    def wrap(i, n):
        return lax.rem(i + n, n)

    pair = {"shot": shot + 1 - 2 * y}
    left, right = {"strip": wrap(strip - 1, strips)}, {"strip": wrap(strip + 1, strips)}
    others = [at_x(wrap(x + d, NUM_X)) for d in range(1, NUM_X)]
    others += [at_z(wrap(z + d, NUM_Z)) for d in range(1, NUM_Z)]
    others += [pair, left, right]
    barrier = pltpu.get_barrier_semaphore()
    for other in others:
        pl.semaphore_signal(barrier, inc=1, device_id=other, device_id_type=MESH)

    def group_z(i):
        return NUM_Z // 2 + i

    def group_x(i, half):
        return 2 * i + half + i // (NUM_X // 2) * NUM_Z

    def own(name, owner, half):
        if name == "z":
            return [(group_z(owner), half * 2 + q) for q in range(2)]
        return [(group_x(owner, half), q) for q in range(4)]

    def terms(place):
        group, q = place
        return img[group, q * QUARTER : (q + 1) * QUARTER]

    plans = {
        "z": (NUM_Z, z, at_z, stage_z, slot_z),
        "x": (NUM_X, x, at_x, stage_x, slot_x),
    }
    arrived = {}
    slots = {}
    for name, (n, *_) in plans.items():
        first = 0
        for c, (_, hops, _) in enumerate(ring_chains(n)):
            slots[name, c] = first
            first += hops
    started = []

    def push(src_ref, dst_ref, device):
        i = len(started)
        copy = pltpu.make_async_remote_copy(
            src_ref=src_ref,
            dst_ref=dst_ref,
            send_sem=send.at[i],
            recv_sem=recv.at[i],
            device_id=device,
            device_id_type=MESH,
        )
        copy.start()
        started.append(copy)
        return copy

    def fill(name, c):
        n, here, _, stage, _ = plans[name]
        way, hops, half = ring_chains(n)[c]
        for q, place in enumerate(own(name, wrap(here + way * hops, n), half)):
            stage[c, q] = encode(terms(place))

    def reduce_step(name, j, c):
        n, here, device, stage, slot = plans[name]
        way, hops, half = ring_chains(n)[c]
        if j > hops:
            return
        held = stage.at[c]
        if j > 1:
            held = slot.at[slots[name, c] + j - 2]
            arrived[name, c].wait_recv()
            for q, place in enumerate(own(name, wrap(here + way * (hops + 1 - j), n), half)):
                held[q] = encode(decode(held[q]) + terms(place))
        arrived[name, c] = push(held, slot.at[slots[name, c] + j - 1], device(wrap(here + way, n)))

    def reduce_end(name, half, q):
        n, here, _, _, slot = plans[name]
        total = terms(own(name, here, half)[q])
        for c, (_, hops, side) in enumerate(ring_chains(n)):
            if side == half:
                total += decode(slot[slots[name, c] + hops - 1, q])
        return total

    unit = unit_matrix(width, width)
    pos = shots_pos[0]

    def inside(first, rows):
        cells = strip * width + first + lax.broadcasted_iota(jnp.int32, (rows, width), 0)
        return jnp.abs(cells - pos) <= width * strips // 4

    def take_in(field, wide, which, mask):
        for t in range(steps):
            value = turned(unit, field[t].reshape(width, width))
            if mask is not None:
                value = jnp.where(mask, value, 0.0)
            wide[t, rim : rim + width] = value
            edge_out[which, 0, t] = value[width - rim :].astype(jnp.bfloat16)
            edge_out[which, 1, t] = value[:rim].astype(jnp.bfloat16)

    def push_edges(which):
        return [push(edge_out.at[which, side], edge_in.at[which, side], (right, left)[side]) for side in range(2)]

    def take_edges(copies, wide, which):
        for copy in copies:
            copy.wait_recv()
        has_left = jnp.full((rim, width), strip, jnp.int32) > 0
        has_right = jnp.full((rim, width), strip, jnp.int32) < strips - 1
        for t in range(steps):
            wide[t, 0:rim] = jnp.where(has_left, edge_in[which, 0, t].astype(F32), 0.0)
            wide[t, rim + width : 2 * rim + width] = jnp.where(has_right, edge_in[which, 1, t].astype(F32), 0.0)

    take_in(rec, rec32, 0, None)
    pl.semaphore_wait(barrier, len(others))
    rec_edges = push_edges(0)
    take_in(src, src32, 1, inside(0, width))
    src_edges = push_edges(1)

    scale = [weight[k].astype(F32) * (1.0 / terms_count) for k in range(count)]
    spread = count + (BATCH - 1) * ROWS

    def uses(low):
        return [(g, low - g * ROWS) for g in range(BATCH) if 0 <= low - g * ROWS < count]

    def correlate(i):
        base = pl.multiple_of(i * BATCH * ROWS, ROWS)
        for first in range(0, steps, SOME):
            mine = [
                [src32[first + t, pl.ds(base + g * ROWS + rim, ROWS)] for t in range(SOME)] for g in range(BATCH)
            ]
            for low in range(spread):
                window = [rec32[first + t, pl.ds(base + low, ROWS)] for t in range(SOME)]
                for g, k in uses(low):
                    total = mine[g][0] * window[0]
                    for t in range(1, SOME):
                        total += mine[g][t] * window[t]
                    at = i * BATCH + g
                    if first > 0:
                        total += img[at, k]
                    img[at, k] = total * scale[k] if first + SOME == steps else total
        for g in range(BATCH):
            for k in range(count, PAD):
                img[i * BATCH + g, k] = jnp.zeros((ROWS, width), F32)

    @pl.loop(1, 3)
    def _(i):
        correlate(i)

    order = (0, 2, 1, 3)
    for c in order:
        fill("z", c)
        reduce_step("z", 1, c)
    take_edges(rec_edges, rec32, 0)

    @pl.loop(0, 2)
    def _(i):
        correlate(i * 3)

    for c in order:
        fill("x", c)
        reduce_step("x", 1, c)
    for c in order:
        reduce_step("z", 2, c)
    take_edges(src_edges, src32, 1)
    for c in order:
        reduce_step("x", 2, c)
    for c in order:
        reduce_step("z", 3, c)
    for c in order:
        arrived["x", c].wait_recv()
    for half in range(2):
        for q in range(4):
            send_x[half * 4 + q] = encode(reduce_end("x", half, q))
    second_x = []
    for d in range(1, NUM_Z):
        other = wrap(z + d, NUM_Z)
        second_x.append(push(send_x.at[other], in_x.at[d - 1], at_z(other)))
    for c in order:
        reduce_step("z", 4, c)
    for c in order:
        arrived["z", c].wait_recv()
    for half in range(2):
        for q in range(2):
            send_z[half * 2 + q] = encode(reduce_end("z", half, q))
    second_z = []
    for d in range(1, NUM_X):
        other = wrap(x + d, NUM_X)
        second_z.append(push(send_z.at[other], in_z.at[d - 1], at_x(other)))

    total = decode(send_x[z])
    for d in range(1, NUM_Z):
        second_x[d - 1].wait_recv()
        total += decode(in_x[d - 1])
    pair_out[0] = encode(total)
    pair_x = push(pair_out.at[0], pair_in.at[0], pair)
    total = decode(send_z[x])
    for d in range(1, NUM_X):
        second_z[d - 1].wait_recv()
        total += decode(in_z[d - 1])
    pair_out[1] = encode(total)
    pair_z = push(pair_out.at[1], pair_in.at[1], pair)

    mine_x = out.at[group_x(x, z // 4), z % 4]
    pair_x.wait_recv()
    mine_x[...] = encode(decode(pair_out[0]) + decode(pair_in[0]))
    third_x = [push(mine_x, mine_x, at_z(wrap(z + d, NUM_Z))) for d in range(1, NUM_Z)]
    mine_z = out.at[group_z(z), x]
    pair_z.wait_recv()
    mine_z[...] = encode(decode(pair_out[1]) + decode(pair_in[1]))
    third_z = [push(mine_z, mine_z, at_x(wrap(x + d, NUM_X))) for d in range(1, NUM_X)]

    def part(name, owner, half):
        if name == "z":
            return out.at[group_z(owner), pl.ds(half * 2, 2)]
        return out.at[group_x(owner, half)]

    def gather_step(name, j, c):
        n, here, device, _, _ = plans[name]
        way, hops, half = ring_chains(n)[c]
        if j > hops + 1:
            return
        if j > 1:
            arrived[name, c].wait_recv()
        if j <= hops:
            held = part(name, wrap(here - way * (j - 1), n), half)
            arrived[name, c] = push(held, held, device(wrap(here + way, n)))

    def unpack(g, start, quarters):
        for q in quarters:
            values = decode(out[g, q])
            for i in range(QUARTER):
                if q * QUARTER + i < count:
                    pen[q * QUARTER + i, pl.ds(start, ROWS)] = values[i]

    def update_source(i):
        base = pl.multiple_of(i * BATCH * ROWS, ROWS)
        for g in range(BATCH):
            unpack(i * BATCH + g, base + g * ROWS + rim, range(4))
        masks = [inside(base + g * ROWS, ROWS) for g in range(BATCH)]
        for first in range(0, steps, SOME):
            total = {}
            for low in range(spread):
                window = [rec32[first + t, pl.ds(base + low, ROWS)] for t in range(SOME)]
                for g, k in uses(low):
                    p = pen[k, pl.ds(base + g * ROWS + rim, ROWS)]
                    for t in range(SOME):
                        term = p * window[t]
                        total[g, t] = term if k == 0 else total[g, t] + term
            for g in range(BATCH):
                for t in range(SOME):
                    held[first + t, pl.ds(base + g * ROWS, ROWS)] = jnp.where(masks[g], total[g, t], 0.0)

    def update_receiver(i):
        base = pl.multiple_of(i * BATCH * ROWS, ROWS)
        for first in range(0, steps, SOME):
            total = {}
            for low in range(spread):
                window = [src32[first + t, pl.ds(base + low, ROWS)] for t in range(SOME)]
                for g, back in uses(low):
                    k = count - 1 - back
                    p = pen[k, pl.ds(base + low, ROWS)]
                    for t in range(SOME):
                        term = p * window[t]
                        total[g, t] = term if back == 0 else total[g, t] + term
            for g in range(BATCH):
                for t in range(SOME):
                    held[first + t, pl.ds(base + g * ROWS, ROWS)] = total[g, t]

    for copy in third_z:
        copy.wait_recv()
    for c in order:
        gather_step("z", 1, c)
    for copy in third_x:
        copy.wait_recv()
    for c in order:
        gather_step("x", 1, c)
    for c in order:
        gather_step("z", 2, c)
    for c in order:
        gather_step("x", 2, c)
    for c in order:
        gather_step("z", 3, c)
    for c in order:
        gather_step("x", 3, c)

    to_right = push(
        out.at[pl.ds(groups - edge, edge), pl.ds(1, 3)],
        out.at[pl.ds(groups, edge), pl.ds(1, 3)],
        right,
    )
    to_left = push(out.at[pl.ds(0, edge), pl.ds(0, 2)], out.at[pl.ds(groups + edge, edge), pl.ds(0, 2)], left)
    for c in order:
        gather_step("z", 4, c)

    @pl.loop(0, 2)
    def _(i):
        update_source(i * 3)

    for c in order:
        gather_step("z", 5, c)

    @pl.loop(1, 3)
    def _(i):
        update_source(i)

    unit_pair = unit_matrix(width, 2 * width)
    for t in range(steps):
        src_upd[t] = turned_pair(unit_pair, held[t]).reshape(src_upd.shape[1:])
    to_right.wait_recv()
    to_left.wait_recv()
    for g in range(edge):
        unpack(groups + g, g * ROWS, range(1, 4))
        unpack(groups + edge + g, rim + width + g * ROWS, range(2))

    @pl.loop(0, groups // BATCH)
    def _(i):
        update_receiver(i)

    for t in range(steps):
        rec_upd[t] = turned_pair(unit_pair, held[t]).reshape(rec_upd.shape[1:])
    for copy in started:
        copy.wait_send()


def local(strips, shots, source_field, receiver_field, shot_pos, offset_weight):
    src, rec = source_field[0], receiver_field[0]
    steps, _, _, width = src.shape
    rim = offset_weight.shape[0] // 2
    span, groups = width + 2 * rim, width // ROWS
    piece = (WORDS, ROWS, width)

    def words(*lead):
        return pltpu.VMEM(lead + piece, jnp.int32)

    wide = pltpu.VMEM((steps, span, width), F32)
    edges = pltpu.VMEM((2, 2, steps, rim, width), jnp.bfloat16)
    upd = jax.ShapeDtypeStruct(src.shape, F32)
    src_upd, rec_upd = pl.pallas_call(
        functools.partial(fused_kernel, strips, float(shots * steps)),
        out_shape=(upd, upd),
        in_specs=[SMEM, SMEM, VMEM, VMEM],
        out_specs=(VMEM, VMEM),
        scratch_shapes=[
            wide,
            wide,
            edges,
            edges,
            pltpu.VMEM((groups, PAD, ROWS, width), F32),
            words(groups + 2 * rim // ROWS, 4),
            pltpu.VMEM((offset_weight.shape[0], span, width), F32),
            pltpu.VMEM((steps, width, width), F32),
            words(4, 2),
            words(4, 4),
            words(2 * NUM_Z - 2, 2),
            words(2 * NUM_X - 2, 4),
            words(4),
            words(8),
            words(NUM_X - 1),
            words(NUM_Z - 1),
            words(2),
            words(2),
            pltpu.SemaphoreType.DMA((80,)),
            pltpu.SemaphoreType.DMA((80,)),
        ],
        compiler_params=pltpu.CompilerParams(
            collective_id=0, has_side_effects=True, vmem_limit_bytes=60 * 2**20
        ),
        name="fused",
    )(shot_pos, offset_weight, rec, src)
    return src_upd[None], rec_upd[None]


def solution(mesh):
    return jax.shard_map(
        functools.partial(local, mesh.shape["strip"], mesh.shape["shot"]),
        mesh=mesh,
        in_specs=(
            P("shot", None, None, None, "strip"),
            P("shot", None, None, None, "strip"),
            P("shot"),
            P(),
        ),
        out_specs=(P("shot", None, None, None, "strip"), P("shot", None, None, None, "strip")),
        check_vma=False,
    )
```

```python
import functools

import jax
import jax.numpy as jnp
from jax import lax
from jax.experimental import pallas as pl
from jax.experimental.pallas import tpu as pltpu
from jax.sharding import PartitionSpec as P

MESH = pl.DeviceIdType.MESH
VMEM = pl.BlockSpec(memory_space=pltpu.VMEM)
SMEM = pl.BlockSpec(memory_space=pltpu.SMEM)
HBM = pl.BlockSpec(memory_space=pltpu.HBM)
F32 = jnp.float32

NUM_X, NUM_Z, NUM_Y = 4, 8, 2
ROWS = 8
BATCH, SOME = 4, 8
PAD = 36
QUARTER = PAD // 4
WORDS = (QUARTER + 1) // 2
TINY, LIMIT, STEPS_2 = 1e-30, 32767.0, 16.0


def unit_matrix(rows, columns):
    i = lax.broadcasted_iota(jnp.int32, (rows, columns), 0)
    j = lax.broadcasted_iota(jnp.int32, (rows, columns), 1)
    return jnp.where(lax.rem(j, rows) == i, 1.0, 0.0).astype(jnp.bfloat16)


def turned(unit, values):
    return lax.dot_general(unit, values, (((1,), (1,)), ((), ())), preferred_element_type=F32)


def turned_pair(unit, values):
    high = values.astype(jnp.bfloat16)
    low = (values - high.astype(F32)).astype(jnp.bfloat16)
    return turned(unit, jnp.concatenate([high, low], axis=1))


def encode(values):
    top = jnp.maximum(jnp.max(jnp.abs(values), axis=0), TINY)
    code = jnp.ceil(jnp.log2(top) * STEPS_2)
    scaled = jnp.round(values * (LIMIT / jnp.exp2(code * (1.0 / STEPS_2))))
    whole = jnp.clip(scaled, -LIMIT, LIMIT).astype(jnp.int32)
    low = jnp.concatenate([whole[WORDS:], code.astype(jnp.int32)[None]])
    return (whole[:WORDS] << 16) | (low & 0xFFFF)


def decode(words):
    high, low = words >> 16, (words << 16) >> 16
    scale = jnp.exp2(low[WORDS - 1].astype(F32) * (1.0 / STEPS_2)) * (1.0 / LIMIT)
    return jnp.concatenate([high, low[: WORDS - 1]]).astype(F32) * scale


def ring_chains(n):
    far, near = n // 2, n // 2 - 1
    ways = [(1, 0), (-1, 2), (1, 1), (-1, 3)]
    return [(way, far, q) for way, q in ways] + [(-way, near, q) for way, q in ways]


def fused_kernel(
    strips,
    terms_count,
    shots_pos,
    rec_hbm,
    src_hbm,
    weight_hbm,
    src_upd,
    rec_upd,
    rec,
    src,
    weight,
    local,
    rec32,
    src32,
    edge_out,
    edge_in,
    img,
    out,
    pen,
    stage_z,
    stage_x,
    slot_z,
    slot_x,
    send_z,
    send_x,
    in_z,
    in_x,
    rim_in,
    send,
    recv,
    plane_send,
    plane_recv,
    rim_send,
    rim_recv,
):
    steps, width = rec.shape[0], rec.shape[-1]
    count = weight.shape[0]
    rim = count // 2
    edge = rim // ROWS
    groups = width // ROWS
    shot, strip = lax.axis_index("shot"), lax.axis_index("strip")
    x, z, y = shot // (NUM_Z * NUM_Y), shot // NUM_Y % NUM_Z, shot % NUM_Y

    def at_x(i):
        return {"shot": (i * NUM_Z + z) * NUM_Y + y}

    def at_z(i):
        return {"shot": (x * NUM_Z + i) * NUM_Y + y}

    def wrap(i, n):
        return lax.rem(i + n, n)

    def at_xy(i, j):
        return {"shot": (i * NUM_Z + z) * NUM_Y + j}

    left, right = {"strip": wrap(strip - 1, strips)}, {"strip": wrap(strip + 1, strips)}
    plane, sources = [], []
    for dx in (2, 1, 3, 0):
        for dy in (1, 0):
            if dx or dy:
                plane.append((wrap(x + dx, NUM_X), y + dy - 2 * dy * y))
                sources.append((wrap(x - dx, NUM_X), y + dy - 2 * dy * y))
    line = [wrap(z + d, NUM_Z) for d in (4, 3, 5, 2, 6, 1, 7)]
    others = [at_xy(*place) for place in plane] + [at_z(i) for i in line] + [left, right]
    barrier = pltpu.get_barrier_semaphore()
    loads = []
    for i, (there, here) in enumerate(((rec_hbm, rec), (src_hbm, src), (weight_hbm, weight))):
        loads.append(pltpu.make_async_copy(there, here, local.at[i]))
        loads[-1].start()
    for other in others:
        pl.semaphore_signal(barrier, inc=1, device_id=other, device_id_type=MESH)

    def group_z(i):
        return NUM_Z // 2 + i

    def group_xy(i, j):
        return NUM_Y * i + j + i // (NUM_X // 2) * NUM_Z

    def terms(group, q):
        return img[group, q * QUARTER : (q + 1) * QUARTER]

    started = []

    def push(src_ref, dst_ref, device):
        i = len(started)
        copy = pltpu.make_async_remote_copy(
            src_ref=src_ref,
            dst_ref=dst_ref,
            send_sem=send.at[i],
            recv_sem=recv.at[i],
            device_id=device,
            device_id_type=MESH,
        )
        copy.start()
        started.append(copy)
        return copy

    chains = ring_chains(NUM_Z)
    firsts = [sum(hops for _, hops, _ in chains[:c]) for c in range(len(chains))]
    arrived = [None] * len(chains)

    def reduce_step(j):
        for c, (way, hops, q) in enumerate(chains):
            if j > hops:
                continue
            group = group_z(wrap(z + way * (hops + 1 - j), NUM_Z))
            if j == 1:
                held_here = stage_z.at[c]
                held_here[...] = encode(terms(group, q))
            else:
                held_here = slot_z.at[firsts[c] + j - 2]
                arrived[c].wait_recv()
                held_here[...] = encode(decode(held_here[...]) + terms(group, q))
            arrived[c] = push(held_here, slot_z.at[firsts[c] + j - 1], at_z(wrap(z + way, NUM_Z)))

    def gather_step(j):
        for c, (way, hops, q) in enumerate(chains):
            if j > hops + 1:
                continue
            if j > 1:
                arrived[c].wait_recv()
            if j <= hops:
                piece = out.at[group_z(wrap(z - way * (j - 1), NUM_Z)), q]
                arrived[c] = push(piece, piece, at_z(wrap(z + way, NUM_Z)))

    unit = unit_matrix(width, width)
    pos = shots_pos[0]

    def inside(first, rows):
        cells = strip * width + first + lax.broadcasted_iota(jnp.int32, (rows, width), 0)
        return jnp.abs(cells - pos) <= width * strips // 4

    def take_in(field, wide, which, mask):
        for t in range(steps):
            value = turned(unit, field[t].reshape(width, width))
            if mask is not None:
                value = jnp.where(mask, value, 0.0)
            wide[t, rim : rim + width] = value
            edge_out[which, 0, t] = value[width - rim :].astype(jnp.bfloat16)
            edge_out[which, 1, t] = value[:rim].astype(jnp.bfloat16)

    def push_edges(which):
        return [push(edge_out.at[which, side], edge_in.at[which, side], (right, left)[side]) for side in range(2)]

    def take_edges(copies, wide, which):
        for copy in copies:
            copy.wait_recv()
        has_left = jnp.full((rim, width), strip, jnp.int32) > 0
        has_right = jnp.full((rim, width), strip, jnp.int32) < strips - 1
        for t in range(steps):
            wide[t, 0:rim] = jnp.where(has_left, edge_in[which, 0, t].astype(F32), 0.0)
            wide[t, rim + width : 2 * rim + width] = jnp.where(has_right, edge_in[which, 1, t].astype(F32), 0.0)

    loads[0].wait()
    take_in(rec, rec32, 0, None)
    pl.semaphore_wait(barrier, len(others))
    rec_edges = push_edges(0)
    loads[1].wait()
    take_in(src, src32, 1, inside(0, width))
    src_edges = push_edges(1)

    loads[2].wait()
    scale = [weight[k].astype(F32) * (1.0 / terms_count) for k in range(count)]

    def uses(low, batch):
        return [(g, low - g * ROWS) for g in range(batch) if 0 <= low - g * ROWS < count]

    def correlate(start, batch):
        base = pl.multiple_of(start * ROWS, ROWS)
        for first in range(0, steps, SOME):
            mine = [
                [src32[first + t, pl.ds(base + g * ROWS + rim, ROWS)] for t in range(SOME)] for g in range(batch)
            ]
            for low in range(count + (batch - 1) * ROWS):
                window = [rec32[first + t, pl.ds(base + low, ROWS)] for t in range(SOME)]
                for g, k in uses(low, batch):
                    total = mine[g][0] * window[0]
                    for t in range(1, SOME):
                        total += mine[g][t] * window[t]
                    if first > 0:
                        total += img[start + g, k]
                    img[start + g, k] = total * scale[k] if first + SOME == steps else total
        for g in range(batch):
            for k in range(count, PAD):
                img[start + g, k] = jnp.zeros((ROWS, width), F32)

    @pl.loop(1, groups // BATCH - 1)
    def _(i):
        correlate(i * BATCH, BATCH)

    reduce_step(1)

    @pl.loop(0, 2)
    def _(i):
        correlate(edge + i * (groups - 3 * edge), edge)

    def place_of(i, far):
        column = lax.rem(x + i // NUM_Y, 2)
        return (3 * column if far else 1 + column), lax.rem(y + i + 1, NUM_Y)

    def order_of(i, j):
        return i * NUM_Y + j

    my_order = order_of(x, y)

    def plane_copy(place):
        return pltpu.make_async_remote_copy(
            src_ref=stage_x.at[order_of(*place)],
            dst_ref=slot_x.at[my_order],
            send_sem=plane_send.at[order_of(*place)],
            recv_sem=plane_recv.at[my_order],
            device_id=at_xy(*place),
            device_id_type=MESH,
        )

    def push_plane(place):
        for q in range(4):
            stage_x[order_of(*place), q] = encode(terms(group_xy(*place), q))

        @pl.when(order_of(*place) != my_order)
        def _():
            plane_copy(place).start()

    every = [(i, j) for i in range(NUM_X) for j in range(NUM_Y)]
    for i in range(NUM_X):
        push_plane(place_of(i, False))
    reduce_step(2)
    take_edges(rec_edges, rec32, 0)

    @pl.loop(0, 2)
    def _(i):
        correlate(i * (groups - edge), edge)

    for i in range(NUM_X):
        push_plane(place_of(i, True))
    reduce_step(3)
    reduce_step(4)

    for q in range(4):
        slot_x[my_order, q] = stage_x[my_order, q]
    for i, place in enumerate(every):

        @pl.when(i != my_order)
        def _():
            pltpu.make_async_remote_copy(
                src_ref=stage_x.at[i],
                dst_ref=slot_x.at[i],
                send_sem=plane_send.at[i],
                recv_sem=plane_recv.at[i],
                device_id=at_xy(*place),
                device_id_type=MESH,
            ).wait()

    for q in range(4):
        total = decode(slot_x[0, q])
        for i in range(1, len(every)):
            total += decode(slot_x[i, q])
        send_x[q] = encode(total)
    second_xy = [push(send_x.at[i % 4], in_x.at[j], at_z(i)) for j, i in enumerate(line)]

    for q in range(4):
        total = terms(group_z(z), q)
        for c, (_, hops, own) in enumerate(chains):
            if own == q:
                arrived[c].wait_recv()
                total += decode(slot_z[firsts[c] + hops - 1])
        send_z[q] = encode(total)
    second_z = [push(send_z.at[i], in_z.at[n], at_xy(i, j)) for n, (i, j) in enumerate(plane)]

    total = decode(send_x[z % 4])
    for j in range(len(line)):
        second_xy[j].wait_recv()
        total += decode(in_x[j])
    mine_xy = out.at[group_xy(x, y), z % 4]
    mine_xy[...] = encode(total)
    third_xy = [push(mine_xy, mine_xy, at_z(wrap(z + d, NUM_Z))) for d in (2, 1, NUM_Z - 1)]
    total = decode(send_z[x])
    for j in range(len(plane)):
        second_z[j].wait_recv()
        total += decode(in_z[j])
    mine_z = out.at[group_z(z), x]
    mine_z[...] = encode(total)
    third_z = [push(mine_z, mine_z, at_x(wrap(x + d, NUM_X))) for d in (2, 1, 3)]

    def unpack(g, start, quarters):
        for q in quarters:
            values = decode(out[g, q])
            for i in range(QUARTER):
                if q * QUARTER + i < count:
                    pen[q * QUARTER + i, pl.ds(start, ROWS)] = values[i]

    def update_source(places):
        @pl.loop(0, len(places))
        def _(i):
            g = places[0]
            for j in range(1, len(places)):
                g = jnp.where(i == j, places[j], g)
            base = pl.multiple_of(g * ROWS, ROWS)
            unpack(g, base + rim, range(4))
            mask = inside(base, ROWS)
            total = [None] * steps
            for k in range(count):
                p = pen[k, pl.ds(base + rim, ROWS)]
                for t in range(steps):
                    term = p * rec32[t, pl.ds(base + k, ROWS)]
                    total[t] = term if k == 0 else total[t] + term
            for t in range(steps):
                src_upd[t, pl.ds(base, ROWS)] = jnp.where(mask, total[t], 0.0)

    def update_receiver(i):
        base = pl.multiple_of(i * BATCH * ROWS, ROWS)
        for first in range(0, steps, SOME):
            total = {}
            for low in range(count + (BATCH - 1) * ROWS):
                window = [src32[first + t, pl.ds(base + low, ROWS)] for t in range(SOME)]
                for g, back in uses(low, BATCH):
                    k = count - 1 - back
                    p = pen[k, pl.ds(base + low, ROWS)]
                    for t in range(SOME):
                        term = p * window[t]
                        total[g, t] = term if back == 0 else total[g, t] + term
            for g in range(BATCH):
                for t in range(SOME):
                    rec_upd[first + t, pl.ds(base + g * ROWS, ROWS)] = total[g, t]

    for copy in third_xy:
        copy.wait_recv()
    whole = out.at[group_xy(x, y)]
    high = x // (NUM_X // 2)
    rim_out = push(
        out.at[group_xy(x, y), pl.ds(high, 3)],
        rim_in,
        {"shot": shot, "strip": wrap(strip - 1 + 2 * high, strips)},
    )
    rim_places = [(i, j) for i in (0, NUM_X - 1) for j in range(NUM_Y)]

    def rim_slot(i, j):
        return groups + i // (NUM_X // 2) * NUM_Y + j

    def rim_copy(place, to, i):
        piece = out.at[rim_slot(*place), pl.ds(place[0] // (NUM_X // 2), 3)]
        return pltpu.make_async_remote_copy(
            src_ref=piece,
            dst_ref=piece,
            send_sem=rim_send.at[i],
            recv_sem=rim_recv.at[order_of(*place)],
            device_id=at_xy(*to),
            device_id_type=MESH,
        )

    def pass_rims():
        rim_out.wait_recv()
        for place in rim_places:

            @pl.when(order_of(*place) == my_order)
            def _():
                for q in range(3):
                    out[rim_slot(*place), place[0] // (NUM_X // 2) + q] = rim_in[q]
                for i, to in enumerate(every):
                    if to != place:
                        rim_copy(place, to, i).start()

    def wait_rims():
        for place in rim_places:

            @pl.when(order_of(*place) == my_order)
            def _():
                for i, to in enumerate(every):
                    if to != place:
                        rim_copy(place, to, i).wait_send()

            @pl.when(order_of(*place) != my_order)
            def _():
                rim_copy(place, place, 0).wait_recv()

    fourth_xy = [push(whole, whole, at_xy(*place)) for place in plane]
    for copy in third_z:
        copy.wait_recv()

    def along(d):
        return group_z(wrap(z + d, NUM_Z))

    def over_plane(first, last):
        for copy in fourth_xy[first:last]:
            copy.wait_recv()
        return [group_xy(*place) for place in sources[first:last]]

    gather_step(1)
    take_edges(src_edges, src32, 1)
    update_source([along(0), group_xy(x, y)])
    gather_step(2)
    update_source([along(1), along(-1)])
    gather_step(3)
    pass_rims()
    update_source([along(2), along(-2)])
    gather_step(4)
    update_source([along(3), along(-3)])
    update_source(over_plane(0, 3))
    gather_step(5)
    update_source(over_plane(3, 7) + [along(4)])

    @pl.loop(1, 3)
    def _(i):
        update_receiver(i)

    wait_rims()
    for g in range(edge):
        unpack(groups + edge + g, g * ROWS, range(1, 4))
        unpack(groups + g, rim + width + g * ROWS, range(2))

    @pl.loop(0, 2)
    def _(i):
        update_receiver(i * 3)

    for copy in started:
        copy.wait_send()


def finish_kernel(src_rows, rec_rows, src_upd, rec_upd, turned_src, turned_rec, done):
    steps, width = src_rows.shape[:2]
    unit_pair = unit_matrix(width, 2 * width)
    copies = []
    for t in range(steps):
        for i, (rows, held, whole) in enumerate(
            ((src_rows, turned_src, src_upd), (rec_rows, turned_rec, rec_upd))
        ):
            held[t] = turned_pair(unit_pair, rows[t]).reshape(held.shape[1:])
            copy = pltpu.make_async_copy(held.at[t], whole.at[t], done.at[i, t])
            copy.start()
            copies.append(copy)
    for copy in copies:
        copy.wait()


def local(strips, shots, source_field, receiver_field, shot_pos, offset_weight):
    src, rec = source_field[0], receiver_field[0]
    steps, _, _, width = src.shape
    rim = offset_weight.shape[0] // 2
    span, groups = width + 2 * rim, width // ROWS
    piece = (WORDS, ROWS, width)

    def words(*lead):
        return pltpu.VMEM(lead + piece, jnp.int32)

    wide = pltpu.VMEM((steps, span, width), F32)
    edges = pltpu.VMEM((2, 2, steps, rim, width), jnp.bfloat16)
    rows = jax.ShapeDtypeStruct((steps, width, width), F32)
    src_rows, rec_rows = pl.pallas_call(
        functools.partial(fused_kernel, strips, float(shots * steps)),
        out_shape=(rows, rows),
        in_specs=[SMEM, HBM, HBM, HBM],
        out_specs=(VMEM, VMEM),
        scratch_shapes=[
            pltpu.VMEM(rec.shape, rec.dtype),
            pltpu.VMEM(src.shape, src.dtype),
            pltpu.SMEM(offset_weight.shape, offset_weight.dtype),
            pltpu.SemaphoreType.DMA((3,)),
            wide,
            wide,
            edges,
            edges,
            pltpu.VMEM((groups, PAD, ROWS, width), F32),
            words(groups + 2 * rim // ROWS, 4),
            pltpu.VMEM((offset_weight.shape[0], span, width), F32),
            words(8),
            words(NUM_X * NUM_Y, 4),
            words(4 * NUM_Z - 4),
            words(NUM_X * NUM_Y, 4),
            words(4),
            words(4),
            words(7),
            words(7),
            words(3),
            pltpu.SemaphoreType.DMA((96,)),
            pltpu.SemaphoreType.DMA((96,)),
            pltpu.SemaphoreType.DMA((NUM_X * NUM_Y,)),
            pltpu.SemaphoreType.DMA((NUM_X * NUM_Y,)),
            pltpu.SemaphoreType.DMA((NUM_X * NUM_Y,)),
            pltpu.SemaphoreType.DMA((NUM_X * NUM_Y,)),
        ],
        compiler_params=pltpu.CompilerParams(
            collective_id=0, has_side_effects=True, vmem_limit_bytes=28 * 2**20
        ),
        name="fused",
    )(shot_pos, rec, src, offset_weight)

    upd = jax.ShapeDtypeStruct(src.shape, F32)
    src_upd, rec_upd = pl.pallas_call(
        finish_kernel,
        out_shape=(upd, upd),
        in_specs=[VMEM, VMEM],
        out_specs=(HBM, HBM),
        scratch_shapes=[
            pltpu.VMEM(src.shape, F32),
            pltpu.VMEM(src.shape, F32),
            pltpu.SemaphoreType.DMA((2, steps)),
        ],
        compiler_params=pltpu.CompilerParams(vmem_limit_bytes=28 * 2**20),
        name="finish",
    )(src_rows, rec_rows)
    return src_upd[None], rec_upd[None]


def solution(mesh):
    return jax.shard_map(
        functools.partial(local, mesh.shape["strip"], mesh.shape["shot"]),
        mesh=mesh,
        in_specs=(
            P("shot", None, None, None, "strip"),
            P("shot", None, None, None, "strip"),
            P("shot"),
            P(),
        ),
        out_specs=(P("shot", None, None, None, "strip"), P("shot", None, None, None, "strip")),
        check_vma=False,
    )
```

```python
import functools

import jax
import jax.numpy as jnp
from jax import lax
from jax.experimental import pallas as pl
from jax.experimental.pallas import tpu as pltpu
from jax.sharding import PartitionSpec as P

MESH = pl.DeviceIdType.MESH
VMEM = pl.BlockSpec(memory_space=pltpu.VMEM)
SMEM = pl.BlockSpec(memory_space=pltpu.SMEM)
HBM = pl.BlockSpec(memory_space=pltpu.HBM)
F32 = jnp.float32

NUM_X, NUM_Z, NUM_Y = 4, 8, 2
ROWS = 8
BATCH, SOME = 4, 8
PAD = 36
QUARTER = PAD // 4
WORDS = (QUARTER + 1) // 2
TINY, LIMIT, STEPS_2 = 1e-30, 32767.0, 16.0


def unit_matrix(rows, columns):
    i = lax.broadcasted_iota(jnp.int32, (rows, columns), 0)
    j = lax.broadcasted_iota(jnp.int32, (rows, columns), 1)
    return jnp.where(lax.rem(j, rows) == i, 1.0, 0.0).astype(jnp.bfloat16)


def turned(unit, values):
    return lax.dot_general(unit, values, (((1,), (1,)), ((), ())), preferred_element_type=F32)


def turned_pair(unit, values):
    high = values.astype(jnp.bfloat16)
    low = (values - high.astype(F32)).astype(jnp.bfloat16)
    return turned(unit, jnp.concatenate([high, low], axis=1))


def slot_of(k, rim):
    return k if k <= rim else k + 1


def encode(values):
    top = jnp.maximum(jnp.max(jnp.abs(values), axis=0), TINY)
    code = jnp.ceil(jnp.log2(top) * STEPS_2)
    scaled = jnp.round(values * (LIMIT / jnp.exp2(code * (1.0 / STEPS_2))))
    whole = jnp.clip(scaled, -LIMIT, LIMIT).astype(jnp.int32)
    low = jnp.concatenate([whole[WORDS:], code.astype(jnp.int32)[None]])
    return (whole[:WORDS] << 16) | (low & 0xFFFF)


def decode(words):
    high, low = words >> 16, (words << 16) >> 16
    scale = jnp.exp2(low[WORDS - 1].astype(F32) * (1.0 / STEPS_2)) * (1.0 / LIMIT)
    return jnp.concatenate([high, low[: WORDS - 1]]).astype(F32) * scale


def fused_kernel(
    strips,
    terms_count,
    shots_pos,
    rec_hbm,
    src_hbm,
    weight_hbm,
    src_upd,
    rec_upd,
    rec,
    src,
    weight,
    local,
    rec32,
    src32,
    edge_out,
    edge_in,
    img,
    out,
    pen,
    stage_z,
    stage_x,
    slot_z,
    slot_x,
    send_z,
    send_x,
    in_z,
    in_x,
    rim_in,
    send,
    recv,
    plane_send,
    plane_recv,
    rim_send,
    rim_recv,
):
    steps, width = rec.shape[0], rec.shape[-1]
    count = weight.shape[0]
    rim = count // 2
    edge = rim // ROWS
    groups = width // ROWS
    shot, strip = lax.axis_index("shot"), lax.axis_index("strip")
    x, z, y = shot // (NUM_Z * NUM_Y), shot // NUM_Y % NUM_Z, shot % NUM_Y

    def at_x(i):
        return {"shot": (i * NUM_Z + z) * NUM_Y + y}

    def at_z(i):
        return {"shot": (x * NUM_Z + i) * NUM_Y + y}

    def wrap(i, n):
        return lax.rem(i + n, n)

    def at_xy(i, j):
        return {"shot": (i * NUM_Z + z) * NUM_Y + j}

    left, right = {"strip": wrap(strip - 1, strips)}, {"strip": wrap(strip + 1, strips)}
    plane, sources = [], []
    for dx in (2, 1, 3, 0):
        for dy in (1, 0):
            if dx or dy:
                plane.append((wrap(x + dx, NUM_X), y + dy - 2 * dy * y))
                sources.append((wrap(x - dx, NUM_X), y + dy - 2 * dy * y))
    line = [wrap(z + d, NUM_Z) for d in (4, 3, 5, 2, 6, 1, 7)]
    others = [at_xy(*place) for place in plane] + [at_z(i) for i in line] + [left, right]
    barrier = pltpu.get_barrier_semaphore()
    loads = []
    for i, (there, here) in enumerate(((rec_hbm, rec), (src_hbm, src), (weight_hbm, weight))):
        loads.append(pltpu.make_async_copy(there, here, local.at[i]))
        loads[-1].start()
    for other in others:
        pl.semaphore_signal(barrier, inc=1, device_id=other, device_id_type=MESH)

    def group_z(i):
        return NUM_Z // 2 + i

    def group_xy(i, j):
        return NUM_Y * i + j + i // (NUM_X // 2) * NUM_Z

    def terms(group, q):
        return img[group, q * QUARTER : (q + 1) * QUARTER]

    started = []

    def push(src_ref, dst_ref, device):
        i = len(started)
        copy = pltpu.make_async_remote_copy(
            src_ref=src_ref,
            dst_ref=dst_ref,
            send_sem=send.at[i],
            recv_sem=recv.at[i],
            device_id=device,
            device_id_type=MESH,
        )
        copy.start()
        started.append(copy)
        return copy

    far = ((1, 0), (-1, 2), (1, 1), (-1, 3))
    near = tuple((-way, q) for way, q in far)

    def z_group(d):
        return group_z(wrap(z + d, NUM_Z))

    def send_z_step(held_here, to, message, c):
        return push(held_here, slot_z.at[message * len(far) + c], at_z(wrap(z + to, NUM_Z)))

    def start_far():
        copies = []
        for c, (way, q) in enumerate(far):
            stage_z[c] = encode(terms(z_group(4 * way), q))
            copies.append(send_z_step(stage_z.at[c], way, 0, c))
        return copies

    def start_near():
        copies = []
        for c, (way, q) in enumerate(near):
            stage_z[4 + c] = encode(terms(z_group(3 * way), q))
            copies.append(send_z_step(stage_z.at[4 + c], way, 4, c))
        return copies

    def go_on(ways, copies, d, message):
        passed = []
        for c, (way, q) in enumerate(ways):
            held_here = slot_z.at[message[0] * len(far) + c]
            copies[c].wait_recv()
            total = decode(held_here[...]) + terms(z_group(d * way), q)
            held_here[...] = encode(total)
            passed.append(send_z_step(held_here, way, message[1], c))
        return passed

    def pass_quarters(ways, copies, d, steps_on):
        passed = [[] for _ in steps_on]
        for c, (way, q) in enumerate(ways):
            if copies is not None:
                copies[c].wait_recv()
            piece = out.at[z_group(-d * way), q]
            for made, to in zip(passed, steps_on):
                made.append(push(piece, piece, at_z(wrap(z + to * way, NUM_Z))))
        return passed

    def land(copies):
        for copy in copies:
            copy.wait_recv()

    unit = unit_matrix(width, width)
    pos = shots_pos[0]

    def inside(first, rows):
        cells = strip * width + first + lax.broadcasted_iota(jnp.int32, (rows, width), 0)
        return jnp.abs(cells - pos) <= width * strips // 4

    def take_in(field, wide, which, mask):
        for t in range(steps):
            value = turned(unit, field[t].reshape(width, width))
            if mask is not None:
                value = jnp.where(mask, value, 0.0)
            wide[t, rim : rim + width] = value
            edge_out[which, 0, t] = value[width - rim :].astype(jnp.bfloat16)
            edge_out[which, 1, t] = value[:rim].astype(jnp.bfloat16)

    def push_edges(which):
        return [push(edge_out.at[which, side], edge_in.at[which, side], (right, left)[side]) for side in range(2)]

    def take_edges(copies, wide, which):
        for copy in copies:
            copy.wait_recv()
        has_left = jnp.full((rim, width), strip, jnp.int32) > 0
        has_right = jnp.full((rim, width), strip, jnp.int32) < strips - 1
        for t in range(steps):
            wide[t, 0:rim] = jnp.where(has_left, edge_in[which, 0, t].astype(F32), 0.0)
            wide[t, rim + width : 2 * rim + width] = jnp.where(has_right, edge_in[which, 1, t].astype(F32), 0.0)

    loads[0].wait()
    take_in(rec, rec32, 0, None)
    pl.semaphore_wait(barrier, len(others))
    rec_edges = push_edges(0)
    loads[1].wait()
    take_in(src, src32, 1, inside(0, width))
    src_edges = push_edges(1)

    loads[2].wait()
    scale = [weight[k].astype(F32) * (1.0 / terms_count) for k in range(count)]

    def uses(low, batch):
        return [(g, low - g * ROWS) for g in range(batch) if 0 <= low - g * ROWS < count]

    def correlate(start, batch):
        base = pl.multiple_of(start * ROWS, ROWS)
        for first in range(0, steps, SOME):
            mine = [
                [src32[first + t, pl.ds(base + g * ROWS + rim, ROWS)] for t in range(SOME)] for g in range(batch)
            ]
            for low in range(count + (batch - 1) * ROWS):
                window = [rec32[first + t, pl.ds(base + low, ROWS)] for t in range(SOME)]
                for g, k in uses(low, batch):
                    total = mine[g][0] * window[0]
                    for t in range(1, SOME):
                        total += mine[g][t] * window[t]
                    if first > 0:
                        total += img[start + g, slot_of(k, rim)]
                    img[start + g, slot_of(k, rim)] = total * scale[k] if first + SOME == steps else total
        for g in range(batch):
            for empty in set(range(PAD)) - {slot_of(k, rim) for k in range(count)}:
                img[start + g, empty] = jnp.zeros((ROWS, width), F32)

    nearer = z // (NUM_Z // 2)
    correlate((2 - nearer) * BATCH, BATCH)
    far_0 = start_far()
    correlate((1 + nearer) * BATCH, BATCH)
    near_0 = start_near()

    @pl.loop(0, 2)
    def _(i):
        correlate(edge + i * (groups - 3 * edge), edge)

    def place_of(i, far):
        column = lax.rem(x + i // NUM_Y, 2)
        return (3 * column if far else 1 + column), lax.rem(y + i + 1, NUM_Y)

    def order_of(i, j):
        return i * NUM_Y + j

    my_order = order_of(x, y)

    def plane_copy(place):
        return pltpu.make_async_remote_copy(
            src_ref=stage_x.at[order_of(*place)],
            dst_ref=slot_x.at[my_order],
            send_sem=plane_send.at[order_of(*place)],
            recv_sem=plane_recv.at[my_order],
            device_id=at_xy(*place),
            device_id_type=MESH,
        )

    def push_plane(place):
        for q in range(4):
            stage_x[order_of(*place), q] = encode(terms(group_xy(*place), q))

        @pl.when(order_of(*place) != my_order)
        def _():
            plane_copy(place).start()

    every = [(i, j) for i in range(NUM_X) for j in range(NUM_Y)]
    for i in range(NUM_X):
        push_plane(place_of(i, False))
    far_1 = go_on(far, far_0, 3, (0, 1))
    near_1 = go_on(near, near_0, 2, (4, 5))
    take_edges(rec_edges, rec32, 0)

    @pl.loop(0, 2)
    def _(i):
        correlate(i * (groups - edge), edge)

    for i in range(NUM_X):
        push_plane(place_of(i, True))
    far_2 = go_on(far, far_1, 2, (1, 2))
    near_2 = go_on(near, near_1, 1, (5, 6))
    far_3 = go_on(far, far_2, 1, (2, 3))

    for q in range(4):
        slot_x[my_order, q] = stage_x[my_order, q]
    for i, place in enumerate(every):

        @pl.when(i != my_order)
        def _():
            pltpu.make_async_remote_copy(
                src_ref=stage_x.at[i],
                dst_ref=slot_x.at[i],
                send_sem=plane_send.at[i],
                recv_sem=plane_recv.at[i],
                device_id=at_xy(*place),
                device_id_type=MESH,
            ).wait()

    for q in range(4):
        total = decode(slot_x[0, q])
        for i in range(1, len(every)):
            total += decode(slot_x[i, q])
        send_x[q] = encode(total)
    second_xy = [push(send_x.at[i % 4], in_x.at[j], at_z(i)) for j, i in enumerate(line)]

    for q in range(4):
        total = terms(group_z(z), q)
        for ways, copies, message in ((far, far_3, 3), (near, near_2, 6)):
            for c, (_, own) in enumerate(ways):
                if own == q:
                    copies[c].wait_recv()
                    total += decode(slot_z[message * len(far) + c])
        send_z[q] = encode(total)
    second_z = [push(send_z.at[i], in_z.at[n], at_xy(i, j)) for n, (i, j) in enumerate(plane)]

    total = decode(send_x[z % 4])
    for j in range(len(line)):
        second_xy[j].wait_recv()
        total += decode(in_x[j])
    mine_xy = out.at[group_xy(x, y), z % 4]
    mine_xy[...] = encode(total)
    third_xy = [push(mine_xy, mine_xy, at_z(wrap(z + d, NUM_Z))) for d in (2, 1, NUM_Z - 1)]
    total = decode(send_z[x])
    for j in range(len(plane)):
        second_z[j].wait_recv()
        total += decode(in_z[j])
    mine_z = out.at[group_z(z), x]
    mine_z[...] = encode(total)
    third_z = [push(mine_z, mine_z, at_x(wrap(x + d, NUM_X))) for d in (2, 1, 3)]

    def unpack(g, start, quarters):
        for q in quarters:
            values = decode(out[g, q])
            for k in range(count):
                if slot_of(k, rim) // QUARTER == q:
                    pen[k, pl.ds(start, ROWS)] = values[slot_of(k, rim) % QUARTER]

    def update_source(places):
        @pl.loop(0, len(places))
        def _(i):
            g = places[0]
            for j in range(1, len(places)):
                g = jnp.where(i == j, places[j], g)
            base = pl.multiple_of(g * ROWS, ROWS)
            unpack(g, base + rim, range(4))
            mask = inside(base, ROWS)
            total = [None] * steps
            for k in range(count):
                p = pen[k, pl.ds(base + rim, ROWS)]
                for t in range(steps):
                    term = p * rec32[t, pl.ds(base + k, ROWS)]
                    total[t] = term if k == 0 else total[t] + term
            for t in range(steps):
                src_upd[t, pl.ds(base, ROWS)] = jnp.where(mask, total[t], 0.0)

    def update_receiver(i):
        base = pl.multiple_of(i * BATCH * ROWS, ROWS)
        for first in range(0, steps, SOME):
            total = {}
            for low in range(count + (BATCH - 1) * ROWS):
                window = [src32[first + t, pl.ds(base + low, ROWS)] for t in range(SOME)]
                for g, back in uses(low, BATCH):
                    k = count - 1 - back
                    p = pen[k, pl.ds(base + low, ROWS)]
                    for t in range(SOME):
                        term = p * window[t]
                        total[g, t] = term if back == 0 else total[g, t] + term
            for g in range(BATCH):
                for t in range(SOME):
                    rec_upd[first + t, pl.ds(base + g * ROWS, ROWS)] = total[g, t]

    for copy in third_xy:
        copy.wait_recv()
    whole = out.at[group_xy(x, y)]
    high = x // (NUM_X // 2)
    rim_out = push(
        out.at[group_xy(x, y), pl.ds(2 * high, 2)],
        rim_in,
        {"shot": shot, "strip": wrap(strip - 1 + 2 * high, strips)},
    )
    rim_places = [(i, j) for i in (0, NUM_X - 1) for j in range(NUM_Y)]

    def rim_slot(i, j):
        return groups + i // (NUM_X // 2) * NUM_Y + j

    def rim_copy(place, to, i):
        piece = out.at[rim_slot(*place), pl.ds(place[0] // (NUM_X // 2) * 2, 2)]
        return pltpu.make_async_remote_copy(
            src_ref=piece,
            dst_ref=piece,
            send_sem=rim_send.at[i],
            recv_sem=rim_recv.at[order_of(*place)],
            device_id=at_xy(*to),
            device_id_type=MESH,
        )

    def pass_rims():
        rim_out.wait_recv()
        for place in rim_places:

            @pl.when(order_of(*place) == my_order)
            def _():
                for q in range(2):
                    out[rim_slot(*place), place[0] // (NUM_X // 2) * 2 + q] = rim_in[q]
                for i, to in enumerate(every):
                    if to != place:
                        rim_copy(place, to, i).start()

    def wait_rims():
        for place in rim_places:

            @pl.when(order_of(*place) == my_order)
            def _():
                for i, to in enumerate(every):
                    if to != place:
                        rim_copy(place, to, i).wait_send()

            @pl.when(order_of(*place) != my_order)
            def _():
                rim_copy(place, place, 0).wait_recv()

    fourth_xy = [push(whole, whole, at_xy(*place)) for place in plane]
    for copy in third_z:
        copy.wait_recv()

    def along(d):
        return group_z(wrap(z + d, NUM_Z))

    def over_plane(first, last):
        for copy in fourth_xy[first:last]:
            copy.wait_recv()
        return [group_xy(*place) for place in sources[first:last]]

    (far_0,) = pass_quarters(far, None, 0, (1,))
    (near_0,) = pass_quarters(near, None, 0, (1,))
    take_edges(src_edges, src32, 1)
    update_source([along(0), group_xy(x, y)])
    far_2, far_1 = pass_quarters(far, far_0, 1, (2, 1))
    (near_1,) = pass_quarters(near, near_0, 1, (1,))
    update_source([along(1), along(-1)])
    (near_2,) = pass_quarters(near, near_1, 2, (1,))
    (far_3,) = pass_quarters(far, far_2, 3, (1,))
    pass_rims()
    land(far_1)
    update_source([along(2), along(-2)])
    land(near_2)
    update_source([along(3), along(-3)])
    land(far_3)
    update_source([along(4)] + over_plane(0, 3))
    update_source(over_plane(3, 7))

    @pl.loop(1, 3)
    def _(i):
        update_receiver(i)

    wait_rims()
    for g in range(edge):
        unpack(groups + edge + g, g * ROWS, range(2, 4))
        unpack(groups + g, rim + width + g * ROWS, range(2))

    @pl.loop(0, 2)
    def _(i):
        update_receiver(i * 3)

    for copy in started:
        copy.wait_send()


def finish_kernel(src_rows, rec_rows, src_upd, rec_upd, turned_src, turned_rec, done):
    steps, width = src_rows.shape[:2]
    unit_pair = unit_matrix(width, 2 * width)
    copies = []
    for t in range(steps):
        for i, (rows, held, whole) in enumerate(
            ((src_rows, turned_src, src_upd), (rec_rows, turned_rec, rec_upd))
        ):
            held[t] = turned_pair(unit_pair, rows[t]).reshape(held.shape[1:])
            copy = pltpu.make_async_copy(held.at[t], whole.at[t], done.at[i, t])
            copy.start()
            copies.append(copy)
    for copy in copies:
        copy.wait()


def local(strips, shots, source_field, receiver_field, shot_pos, offset_weight):
    src, rec = source_field[0], receiver_field[0]
    steps, _, _, width = src.shape
    rim = offset_weight.shape[0] // 2
    span, groups = width + 2 * rim, width // ROWS
    piece = (WORDS, ROWS, width)

    def words(*lead):
        return pltpu.VMEM(lead + piece, jnp.int32)

    wide = pltpu.VMEM((steps, span, width), F32)
    edges = pltpu.VMEM((2, 2, steps, rim, width), jnp.bfloat16)
    rows = pltpu.VMEM((steps, width, width), F32)
    src_rows, rec_rows = pl.pallas_call(
        functools.partial(fused_kernel, strips, float(shots * steps)),
        out_shape=(rows, rows),
        in_specs=[SMEM, HBM, HBM, HBM],
        out_specs=(VMEM, VMEM),
        scratch_shapes=[
            pltpu.VMEM(rec.shape, rec.dtype),
            pltpu.VMEM(src.shape, src.dtype),
            pltpu.SMEM(offset_weight.shape, offset_weight.dtype),
            pltpu.SemaphoreType.DMA((3,)),
            wide,
            wide,
            edges,
            edges,
            pltpu.VMEM((groups, PAD, ROWS, width), F32),
            words(groups + 2 * rim // ROWS, 4),
            pltpu.VMEM((offset_weight.shape[0], span, width), F32),
            words(8),
            words(NUM_X * NUM_Y, 4),
            words(4 * NUM_Z - 4),
            words(NUM_X * NUM_Y, 4),
            words(4),
            words(4),
            words(7),
            words(7),
            words(2),
            pltpu.SemaphoreType.DMA((96,)),
            pltpu.SemaphoreType.DMA((96,)),
            pltpu.SemaphoreType.DMA((NUM_X * NUM_Y,)),
            pltpu.SemaphoreType.DMA((NUM_X * NUM_Y,)),
            pltpu.SemaphoreType.DMA((NUM_X * NUM_Y,)),
            pltpu.SemaphoreType.DMA((NUM_X * NUM_Y,)),
        ],
        compiler_params=pltpu.CompilerParams(
            collective_id=0, has_side_effects=True, vmem_limit_bytes=56 * 2**20
        ),
        name="fused",
    )(shot_pos, rec, src, offset_weight)

    upd = jax.ShapeDtypeStruct(src.shape, F32)
    src_upd, rec_upd = pl.pallas_call(
        finish_kernel,
        out_shape=(upd, upd),
        in_specs=[VMEM, VMEM],
        out_specs=(HBM, HBM),
        scratch_shapes=[
            pltpu.VMEM(src.shape, F32),
            pltpu.VMEM(src.shape, F32),
            pltpu.SemaphoreType.DMA((2, steps)),
        ],
        compiler_params=pltpu.CompilerParams(vmem_limit_bytes=28 * 2**20),
        name="finish",
    )(src_rows, rec_rows)
    return src_upd[None], rec_upd[None]


def solution(mesh):
    return jax.shard_map(
        functools.partial(local, mesh.shape["strip"], mesh.shape["shot"]),
        mesh=mesh,
        in_specs=(
            P("shot", None, None, None, "strip"),
            P("shot", None, None, None, "strip"),
            P("shot"),
            P(),
        ),
        out_specs=(P("shot", None, None, None, "strip"), P("shot", None, None, None, "strip")),
        check_vma=False,
    )
```

```python
import functools

import jax
import jax.numpy as jnp
from jax import lax
from jax.experimental import pallas as pl
from jax.experimental.pallas import tpu as pltpu
from jax.sharding import PartitionSpec as P

MESH = pl.DeviceIdType.MESH
VMEM = pl.BlockSpec(memory_space=pltpu.VMEM)
SMEM = pl.BlockSpec(memory_space=pltpu.SMEM)
HBM = pl.BlockSpec(memory_space=pltpu.HBM)
F32 = jnp.float32

NUM_X, NUM_Z, NUM_Y = 4, 8, 2
ROWS = 8
BATCH, SOME = 4, 8
PAD = 36
QUARTER = PAD // 4
WORDS = (QUARTER + 1) // 2
TINY, LIMIT, STEPS_2 = 1e-30, 32767.0, 16.0


def unit_matrix(rows, columns):
    i = lax.broadcasted_iota(jnp.int32, (rows, columns), 0)
    j = lax.broadcasted_iota(jnp.int32, (rows, columns), 1)
    return jnp.where(lax.rem(j, rows) == i, 1.0, 0.0).astype(jnp.bfloat16)


def turned(unit, values):
    return lax.dot_general(unit, values, (((1,), (1,)), ((), ())), preferred_element_type=F32)


def turned_pair(unit, values):
    high = values.astype(jnp.bfloat16)
    low = (values - high.astype(F32)).astype(jnp.bfloat16)
    return turned(unit, jnp.concatenate([high, low], axis=1))


def slot_of(k, rim):
    return k if k <= rim else k + 1


def encode(values):
    top = jnp.maximum(jnp.max(jnp.abs(values), axis=0), TINY)
    code = jnp.ceil(jnp.log2(top) * STEPS_2)
    scaled = jnp.round(values * (LIMIT / jnp.exp2(code * (1.0 / STEPS_2))))
    whole = jnp.clip(scaled, -LIMIT, LIMIT).astype(jnp.int32)
    low = jnp.concatenate([whole[WORDS:], code.astype(jnp.int32)[None]])
    return (whole[:WORDS] << 16) | (low & 0xFFFF)


def decode(words):
    high, low = words >> 16, (words << 16) >> 16
    scale = jnp.exp2(low[WORDS - 1].astype(F32) * (1.0 / STEPS_2)) * (1.0 / LIMIT)
    return jnp.concatenate([high, low[: WORDS - 1]]).astype(F32) * scale


def fused_kernel(
    strips,
    terms_count,
    shots_pos,
    rec_hbm,
    src_hbm,
    weight_hbm,
    src_upd,
    rec_upd,
    rec,
    src,
    weight,
    local,
    rec32,
    src32,
    edge_out,
    edge_in,
    img,
    out,
    pen,
    stage_z,
    stage_x,
    slot_z,
    slot_x,
    send_z,
    send_x,
    in_z,
    in_x,
    rim_in,
    send,
    recv,
    plane_send,
    plane_recv,
    rim_send,
    rim_recv,
):
    steps, width = rec.shape[0], rec.shape[-1]
    count = weight.shape[0]
    rim = count // 2
    edge = rim // ROWS
    groups = width // ROWS
    shot, strip = lax.axis_index("shot"), lax.axis_index("strip")
    x, z, y = shot // (NUM_Z * NUM_Y), shot // NUM_Y % NUM_Z, shot % NUM_Y

    def at_x(i):
        return {"shot": (i * NUM_Z + z) * NUM_Y + y}

    def at_z(i):
        return {"shot": (x * NUM_Z + i) * NUM_Y + y}

    def wrap(i, n):
        return lax.rem(i + n, n)

    def at_xy(i, j):
        return {"shot": (i * NUM_Z + z) * NUM_Y + j}

    left, right = {"strip": wrap(strip - 1, strips)}, {"strip": wrap(strip + 1, strips)}
    plane, sources = [], []
    for dx in (2, 1, 3, 0):
        for dy in (1, 0):
            if dx or dy:
                plane.append((wrap(x + dx, NUM_X), y + dy - 2 * dy * y))
                sources.append((wrap(x - dx, NUM_X), y + dy - 2 * dy * y))
    line = [wrap(z + d, NUM_Z) for d in (4, 3, 5, 2, 6, 1, 7)]
    others = [at_xy(*place) for place in plane] + [at_z(i) for i in line] + [left, right]
    barrier = pltpu.get_barrier_semaphore()
    loads = []
    for i, (there, here) in enumerate(((rec_hbm, rec), (src_hbm, src), (weight_hbm, weight))):
        loads.append(pltpu.make_async_copy(there, here, local.at[i]))
        loads[-1].start()
    for other in others:
        pl.semaphore_signal(barrier, inc=1, device_id=other, device_id_type=MESH)

    def group_z(i):
        return NUM_Z // 2 + i

    def group_xy(i, j):
        return NUM_Y * i + j + i // (NUM_X // 2) * NUM_Z

    def terms(group, q):
        return img[group, q * QUARTER : (q + 1) * QUARTER]

    started = []

    def push(src_ref, dst_ref, device):
        i = len(started)
        copy = pltpu.make_async_remote_copy(
            src_ref=src_ref,
            dst_ref=dst_ref,
            send_sem=send.at[i],
            recv_sem=recv.at[i],
            device_id=device,
            device_id_type=MESH,
        )
        copy.start()
        started.append(copy)
        return copy

    far = ((1, 0), (-1, 2), (1, 1), (-1, 3))
    near = tuple((-way, q) for way, q in far)

    def z_group(d):
        return group_z(wrap(z + d, NUM_Z))

    def send_z_step(held_here, to, message, c):
        return push(held_here, slot_z.at[message * len(far) + c], at_z(wrap(z + to, NUM_Z)))

    def start_far():
        copies = []
        for c, (way, q) in enumerate(far):
            stage_z[c] = encode(terms(z_group(4 * way), q))
            copies.append(send_z_step(stage_z.at[c], way, 0, c))
        return copies

    def start_near():
        copies = []
        for c, (way, q) in enumerate(near):
            stage_z[4 + c] = encode(terms(z_group(3 * way), q))
            copies.append(send_z_step(stage_z.at[4 + c], way, 4, c))
        return copies

    def go_on(ways, copies, d, message):
        passed = []
        for c, (way, q) in enumerate(ways):
            held_here = slot_z.at[message[0] * len(far) + c]
            copies[c].wait_recv()
            total = decode(held_here[...]) + terms(z_group(d * way), q)
            held_here[...] = encode(total)
            passed.append(send_z_step(held_here, way, message[1], c))
        return passed

    def pass_quarters(ways, copies, d, steps_on):
        passed = [[] for _ in steps_on]
        for c, (way, q) in enumerate(ways):
            if copies is not None:
                copies[c].wait_recv()
            piece = out.at[z_group(-d * way), q]
            for made, to in zip(passed, steps_on):
                made.append(push(piece, piece, at_z(wrap(z + to * way, NUM_Z))))
        return passed

    def land(copies):
        for copy in copies:
            copy.wait_recv()

    unit = unit_matrix(width, width)
    pos = shots_pos[0]

    def inside(first, rows):
        cells = strip * width + first + lax.broadcasted_iota(jnp.int32, (rows, width), 0)
        return jnp.abs(cells - pos) <= width * strips // 4

    def take_in(field, wide, which, mask):
        for t in range(steps):
            value = turned(unit, field[t].reshape(width, width))
            if mask is not None:
                value = jnp.where(mask, value, 0.0)
            wide[t, rim : rim + width] = value
            edge_out[which, 0, t] = value[width - rim :].astype(jnp.bfloat16)
            edge_out[which, 1, t] = value[:rim].astype(jnp.bfloat16)

    def push_edges(which):
        return [push(edge_out.at[which, side], edge_in.at[which, side], (right, left)[side]) for side in range(2)]

    def take_edges(copies, wide, which):
        for copy in copies:
            copy.wait_recv()
        has_left = jnp.full((rim, width), strip, jnp.int32) > 0
        has_right = jnp.full((rim, width), strip, jnp.int32) < strips - 1
        for t in range(steps):
            wide[t, 0:rim] = jnp.where(has_left, edge_in[which, 0, t].astype(F32), 0.0)
            wide[t, rim + width : 2 * rim + width] = jnp.where(has_right, edge_in[which, 1, t].astype(F32), 0.0)

    loads[0].wait()
    take_in(rec, rec32, 0, None)
    pl.semaphore_wait(barrier, len(others))
    rec_edges = push_edges(0)
    loads[1].wait()
    take_in(src, src32, 1, inside(0, width))
    src_edges = push_edges(1)

    loads[2].wait()
    scale = [weight[k].astype(F32) * (1.0 / terms_count) for k in range(count)]

    def uses(low, batch):
        return [(g, low - g * ROWS) for g in range(batch) if 0 <= low - g * ROWS < count]

    def correlate(start, batch):
        base = pl.multiple_of(start * ROWS, ROWS)
        for first in range(0, steps, SOME):
            mine = [
                [src32[first + t, pl.ds(base + g * ROWS + rim, ROWS)] for t in range(SOME)] for g in range(batch)
            ]
            for low in range(count + (batch - 1) * ROWS):
                window = [rec32[first + t, pl.ds(base + low, ROWS)] for t in range(SOME)]
                for g, k in uses(low, batch):
                    total = mine[g][0] * window[0]
                    for t in range(1, SOME):
                        total += mine[g][t] * window[t]
                    if first > 0:
                        total += img[start + g, slot_of(k, rim)]
                    img[start + g, slot_of(k, rim)] = total * scale[k] if first + SOME == steps else total
        for g in range(batch):
            for empty in set(range(PAD)) - {slot_of(k, rim) for k in range(count)}:
                img[start + g, empty] = jnp.zeros((ROWS, width), F32)

    nearer = z // (NUM_Z // 2)
    correlate((2 - nearer) * BATCH, BATCH)
    far_0 = start_far()
    correlate((1 + nearer) * BATCH, BATCH)
    near_0 = start_near()

    @pl.loop(0, 2)
    def _(i):
        correlate(edge + i * (groups - 3 * edge), edge)

    def place_of(i, far):
        column = lax.rem(x + i // NUM_Y, 2)
        return (3 * column if far else 1 + column), lax.rem(y + i + 1, NUM_Y)

    def order_of(i, j):
        return i * NUM_Y + j

    my_order = order_of(x, y)

    def plane_copy(place):
        return pltpu.make_async_remote_copy(
            src_ref=stage_x.at[order_of(*place)],
            dst_ref=slot_x.at[my_order],
            send_sem=plane_send.at[order_of(*place)],
            recv_sem=plane_recv.at[my_order],
            device_id=at_xy(*place),
            device_id_type=MESH,
        )

    def push_plane(place):
        for q in range(4):
            stage_x[order_of(*place), q] = encode(terms(group_xy(*place), q))

        @pl.when(order_of(*place) != my_order)
        def _():
            plane_copy(place).start()

    every = [(i, j) for i in range(NUM_X) for j in range(NUM_Y)]
    for i in range(NUM_X):
        push_plane(place_of(i, False))
    far_1 = go_on(far, far_0, 3, (0, 1))
    near_1 = go_on(near, near_0, 2, (4, 5))
    take_edges(rec_edges, rec32, 0)

    @pl.loop(0, 2)
    def _(i):
        correlate(i * (groups - edge), edge)

    for i in range(NUM_X):
        push_plane(place_of(i, True))
    far_2 = go_on(far, far_1, 2, (1, 2))
    near_2 = go_on(near, near_1, 1, (5, 6))
    far_3 = go_on(far, far_2, 1, (2, 3))

    for q in range(4):
        slot_x[my_order, q] = stage_x[my_order, q]
    for i, place in enumerate(every):

        @pl.when(i != my_order)
        def _():
            pltpu.make_async_remote_copy(
                src_ref=stage_x.at[i],
                dst_ref=slot_x.at[i],
                send_sem=plane_send.at[i],
                recv_sem=plane_recv.at[i],
                device_id=at_xy(*place),
                device_id_type=MESH,
            ).wait()

    for q in range(4):
        total = decode(slot_x[0, q])
        for i in range(1, len(every)):
            total += decode(slot_x[i, q])
        send_x[q] = encode(total)
    second_xy = [push(send_x.at[i % 4], in_x.at[j], at_z(i)) for j, i in enumerate(line)]

    for q in range(4):
        total = terms(group_z(z), q)
        for ways, copies, message in ((far, far_3, 3), (near, near_2, 6)):
            for c, (_, own) in enumerate(ways):
                if own == q:
                    copies[c].wait_recv()
                    total += decode(slot_z[message * len(far) + c])
        send_z[q] = encode(total)
    second_z = [push(send_z.at[i], in_z.at[n], at_xy(i, j)) for n, (i, j) in enumerate(plane)]

    total = decode(send_x[z % 4])
    for j in range(len(line)):
        second_xy[j].wait_recv()
        total += decode(in_x[j])
    mine_xy = out.at[group_xy(x, y), z % 4]
    mine_xy[...] = encode(total)
    third_xy = [push(mine_xy, mine_xy, at_z(wrap(z + d, NUM_Z))) for d in (2, 1, NUM_Z - 1)]
    total = decode(send_z[x])
    for j in range(len(plane)):
        second_z[j].wait_recv()
        total += decode(in_z[j])
    mine_z = out.at[group_z(z), x]
    mine_z[...] = encode(total)
    third_z = [push(mine_z, mine_z, at_x(wrap(x + d, NUM_X))) for d in (2, 1, 3)]

    def unpack(g, start, quarters):
        for q in quarters:
            values = decode(out[g, q])
            for k in range(count):
                if slot_of(k, rim) // QUARTER == q:
                    pen[k, pl.ds(start, ROWS)] = values[slot_of(k, rim) % QUARTER]

    def update_source(places):
        @pl.loop(0, len(places))
        def _(i):
            g = places[0]
            for j in range(1, len(places)):
                g = jnp.where(i == j, places[j], g)
            base = pl.multiple_of(g * ROWS, ROWS)
            unpack(g, base + rim, range(4))
            mask = inside(base, ROWS)
            total = [None] * steps
            for k in range(count):
                p = pen[k, pl.ds(base + rim, ROWS)]
                for t in range(steps):
                    term = p * rec32[t, pl.ds(base + k, ROWS)]
                    total[t] = term if k == 0 else total[t] + term
            for t in range(steps):
                src_upd[t, pl.ds(base, ROWS)] = jnp.where(mask, total[t], 0.0)

    def update_receiver(i):
        base = pl.multiple_of(i * BATCH * ROWS, ROWS)
        for first in range(0, steps, SOME):
            total = {}
            for low in range(count + (BATCH - 1) * ROWS):
                window = [src32[first + t, pl.ds(base + low, ROWS)] for t in range(SOME)]
                for g, back in uses(low, BATCH):
                    k = count - 1 - back
                    p = pen[k, pl.ds(base + low, ROWS)]
                    for t in range(SOME):
                        term = p * window[t]
                        total[g, t] = term if back == 0 else total[g, t] + term
            for g in range(BATCH):
                for t in range(SOME):
                    rec_upd[first + t, pl.ds(base + g * ROWS, ROWS)] = total[g, t]

    for copy in third_xy:
        copy.wait_recv()
    whole = out.at[group_xy(x, y)]
    high = x // (NUM_X // 2)
    rim_out = push(
        out.at[group_xy(x, y), pl.ds(2 * high, 2)],
        rim_in,
        {"shot": shot, "strip": wrap(strip - 1 + 2 * high, strips)},
    )
    rim_places = [(i, j) for i in (0, NUM_X - 1) for j in range(NUM_Y)]

    def rim_slot(i, j):
        return groups + i // (NUM_X // 2) * NUM_Y + j

    def rim_copy(place, to, i):
        piece = out.at[rim_slot(*place), pl.ds(place[0] // (NUM_X // 2) * 2, 2)]
        return pltpu.make_async_remote_copy(
            src_ref=piece,
            dst_ref=piece,
            send_sem=rim_send.at[i],
            recv_sem=rim_recv.at[order_of(*place)],
            device_id=at_xy(*to),
            device_id_type=MESH,
        )

    def pass_rims():
        rim_out.wait_recv()
        for place in rim_places:

            @pl.when(order_of(*place) == my_order)
            def _():
                for q in range(2):
                    out[rim_slot(*place), place[0] // (NUM_X // 2) * 2 + q] = rim_in[q]
                for i, to in enumerate(every):
                    if to != place:
                        rim_copy(place, to, i).start()

    def wait_rims():
        for place in rim_places:

            @pl.when(order_of(*place) == my_order)
            def _():
                for i, to in enumerate(every):
                    if to != place:
                        rim_copy(place, to, i).wait_send()

            @pl.when(order_of(*place) != my_order)
            def _():
                rim_copy(place, place, 0).wait_recv()

    fourth_xy = [push(whole, whole, at_xy(*place)) for place in plane]
    for copy in third_z:
        copy.wait_recv()

    def along(d):
        return group_z(wrap(z + d, NUM_Z))

    def over_plane(first, last):
        for copy in fourth_xy[first:last]:
            copy.wait_recv()
        return [group_xy(*place) for place in sources[first:last]]

    (far_0,) = pass_quarters(far, None, 0, (1,))
    (near_0,) = pass_quarters(near, None, 0, (1,))
    take_edges(src_edges, src32, 1)
    update_source([along(0), group_xy(x, y)])
    far_2, far_1 = pass_quarters(far, far_0, 1, (2, 1))
    (near_1,) = pass_quarters(near, near_0, 1, (1,))
    update_source([along(1), along(-1)])
    pass_rims()
    (near_2,) = pass_quarters(near, near_1, 2, (1,))
    (far_3,) = pass_quarters(far, far_2, 3, (1,))
    land(far_1)
    update_source([along(2), along(-2)])
    land(near_2)
    update_source([along(3), along(-3)])
    land(far_3)
    update_source([along(4)] + over_plane(0, 3))
    update_source(over_plane(3, 7))

    @pl.loop(1, 3)
    def _(i):
        update_receiver(i)

    wait_rims()
    for g in range(edge):
        unpack(groups + edge + g, g * ROWS, range(2, 4))
        unpack(groups + g, rim + width + g * ROWS, range(2))

    @pl.loop(0, 2)
    def _(i):
        update_receiver(i * 3)

    for copy in started:
        copy.wait_send()


def finish_kernel(src_rows, rec_rows, src_upd, rec_upd, turned_src, turned_rec, done):
    steps, width = src_rows.shape[:2]
    unit_pair = unit_matrix(width, 2 * width)
    copies = []
    for t in range(steps):
        for i, (rows, held, whole) in enumerate(
            ((src_rows, turned_src, src_upd), (rec_rows, turned_rec, rec_upd))
        ):
            held[t] = turned_pair(unit_pair, rows[t]).reshape(held.shape[1:])
            copy = pltpu.make_async_copy(held.at[t], whole.at[t], done.at[i, t])
            copy.start()
            copies.append(copy)
    for copy in copies:
        copy.wait()


def local(strips, shots, source_field, receiver_field, shot_pos, offset_weight):
    src, rec = source_field[0], receiver_field[0]
    steps, _, _, width = src.shape
    rim = offset_weight.shape[0] // 2
    span, groups = width + 2 * rim, width // ROWS
    piece = (WORDS, ROWS, width)

    def words(*lead):
        return pltpu.VMEM(lead + piece, jnp.int32)

    wide = pltpu.VMEM((steps, span, width), F32)
    edges = pltpu.VMEM((2, 2, steps, rim, width), jnp.bfloat16)
    rows = pltpu.VMEM((steps, width, width), F32)
    src_rows, rec_rows = pl.pallas_call(
        functools.partial(fused_kernel, strips, float(shots * steps)),
        out_shape=(rows, rows),
        in_specs=[SMEM, HBM, HBM, HBM],
        out_specs=(VMEM, VMEM),
        scratch_shapes=[
            pltpu.VMEM(rec.shape, rec.dtype),
            pltpu.VMEM(src.shape, src.dtype),
            pltpu.SMEM(offset_weight.shape, offset_weight.dtype),
            pltpu.SemaphoreType.DMA((3,)),
            wide,
            wide,
            edges,
            edges,
            pltpu.VMEM((groups, PAD, ROWS, width), F32),
            words(groups + 2 * rim // ROWS, 4),
            pltpu.VMEM((offset_weight.shape[0], span, width), F32),
            words(8),
            words(NUM_X * NUM_Y, 4),
            words(4 * NUM_Z - 4),
            words(NUM_X * NUM_Y, 4),
            words(4),
            words(4),
            words(7),
            words(7),
            words(2),
            pltpu.SemaphoreType.DMA((96,)),
            pltpu.SemaphoreType.DMA((96,)),
            pltpu.SemaphoreType.DMA((NUM_X * NUM_Y,)),
            pltpu.SemaphoreType.DMA((NUM_X * NUM_Y,)),
            pltpu.SemaphoreType.DMA((NUM_X * NUM_Y,)),
            pltpu.SemaphoreType.DMA((NUM_X * NUM_Y,)),
        ],
        compiler_params=pltpu.CompilerParams(
            collective_id=0, has_side_effects=True, vmem_limit_bytes=56 * 2**20
        ),
        name="fused",
    )(shot_pos, rec, src, offset_weight)

    upd = jax.ShapeDtypeStruct(src.shape, F32)
    src_upd, rec_upd = pl.pallas_call(
        finish_kernel,
        out_shape=(upd, upd),
        in_specs=[VMEM, VMEM],
        out_specs=(HBM, HBM),
        scratch_shapes=[
            pltpu.VMEM(src.shape, F32),
            pltpu.VMEM(src.shape, F32),
            pltpu.SemaphoreType.DMA((2, steps)),
        ],
        compiler_params=pltpu.CompilerParams(vmem_limit_bytes=28 * 2**20),
        name="finish",
    )(src_rows, rec_rows)
    return src_upd[None], rec_upd[None]


def solution(mesh):
    return jax.shard_map(
        functools.partial(local, mesh.shape["strip"], mesh.shape["shot"]),
        mesh=mesh,
        in_specs=(
            P("shot", None, None, None, "strip"),
            P("shot", None, None, None, "strip"),
            P("shot"),
            P(),
        ),
        out_specs=(P("shot", None, None, None, "strip"), P("shot", None, None, None, "strip")),
        check_vma=False,
    )
```
